32 devices in a mesh: mode: 2 (over x), band: 16 (over z, y, core).
Axes of the slice: x: 2, y: 2, z: 4, core: 2. Of those that a mesh axis runs over, the one named last changes fastest.
Arguments:
- mode_field: bfloat16 [2, 4096, 2, 4096], P('mode', 'band'), may hold values from -6 to 6
- figure: bfloat16 [4096, 4096], P('band'), may hold values from -6 to 6
- target: bfloat16 [4096, 4096], P('band'), may hold values from 0 to 2
- footprint: int32 [16, 64], replicated, may hold values from 0 to 1023, as said below
- approach_tiles: bfloat16 [3, 2, 128, 128], replicated, may hold values from -0.21875 to 0.21875
- focus_tiles: bfloat16 [3, 2, 128, 128], replicated, may hold values from -0.21875 to 0.21875
Outputs:
- sensitivity: float32 [4096, 4096], P('band')
The draws below stay inside these ranges and needn't reach their ends.
Inputs may be any that keep to these rules, and one draw needn't show every extreme that they name: `footprint`: entry [d, j] is the surface tile band * 64 + block read by beam tile j of band d; for every beam band d and surface band s at most 8 entries of row d name band s, and some row reaches 8 in every draw.
All inputs are finite; a program needn't handle non-finite values.
Results may differ from the reference program's by a relative error of at most 0.0082.
Values may be sent and summed in bfloat16 or wider, within the bound.
A program may use at most 128 MiB of HBM per device.

```python
import jax
import jax.numpy as jnp
from jax import lax

GRID_CELLS = 4096
TILE = 128
MIRROR_TILE = 64
MODES = 2
BAND_TOTAL = 16
BAND_ROWS = 256
MIRROR_BLOCKS = 64
CAP = 8


def draw_footprint(key, part):
    count_of_bands = BAND_TOTAL
    mirror_block_list = MIRROR_BLOCKS
    raw_start = jax.random.randint(jax.random.fold_in(key, 11), (count_of_bands,), 0, count_of_bands)
    start_band = raw_start * raw_start // count_of_bands
    start_band = start_band.at[count_of_bands - 1].set(count_of_bands - 1)
    shift_draw = jax.random.randint(jax.random.fold_in(key, 12), (count_of_bands,), 0, CAP)
    shift_draw = shift_draw * (jnp.arange(count_of_bands) > 0).astype(jnp.int32)
    column = jnp.arange(mirror_block_list, dtype=jnp.int32)
    advance = (column[None, :] + shift_draw[:, None]) // CAP
    source_band = (start_band[:, None] + advance) % count_of_bands
    source_block = jax.random.randint(jax.random.fold_in(key, 13), (count_of_bands, mirror_block_list), 0, mirror_block_list)
    return (source_band * mirror_block_list + source_block).astype(jnp.int32)


def steps_of(key, extent, split, smallest, top_value):
    factor_of = 1.0
    for axis_at, blocks in split:
        heights = jax.random.uniform(jax.random.fold_in(jax.random.fold_in(key, 6), axis_at), (blocks,), jnp.float32, smallest / len(split), top_value / len(split))
        factor_of = factor_of * jnp.repeat(jnp.exp(heights), extent[axis_at] // blocks).reshape((-1,) + (1,) * (len(extent) - 1 - axis_at))
    return factor_of


def scatter_about(own_key, extent, scale, most, cuts=(), held_as=jnp.bfloat16):
    result = scale * jax.random.normal(own_key, extent, jnp.float32)
    if cuts:
        result = result * steps_of(own_key, extent, cuts, -0.22, 0.18)
    return jnp.clip(result, -most, most).astype(held_as)


def setup_inputs(seed: int = 0) -> dict:
    key_list = jax.random.split(jax.random.key(seed), 7)
    mode_field = scatter_about(key_list[0], (MODES, GRID_CELLS, 2, GRID_CELLS), (1.0 / (2 * MODES) ** 0.5), 6.0, ((0, 2), (1, 16)))
    figure = scatter_about(key_list[1], (GRID_CELLS, GRID_CELLS), 0.5, 6.0, ((0, 16),))
    target = jnp.clip(2.0 * jax.random.uniform(key_list[2], (GRID_CELLS, GRID_CELLS), jnp.float32) ** steps_of(key_list[2], (GRID_CELLS, GRID_CELLS), ((0, 16),), -0.2, 0.2), 0.0, 2.0).astype(jnp.bfloat16)
    footprint = draw_footprint(jax.random.fold_in(key_list[6], 71), 0)
    approach_tiles = scatter_about(key_list[4], (3, 2, TILE, TILE), (6 * TILE) ** -0.5, 0.21875)
    focus_tiles = scatter_about(key_list[5], (3, 2, TILE, TILE), (6 * TILE) ** -0.5, 0.21875)
    return dict(mode_field=mode_field, figure=figure, target=target, footprint=footprint, approach_tiles=approach_tiles, focus_tiles=focus_tiles)


PHASE_FACTOR = 4.0


def real_kernels(tile_set):
    tile_set = tile_set.astype(jnp.float32)
    real_part = tile_set[:, 0]
    imag_part = tile_set[:, 1]
    upper = jnp.stack([real_part, imag_part], axis=2)
    lower = jnp.stack([-imag_part, real_part], axis=2)
    return jnp.stack([upper, lower], axis=1)


def banded(grid_field, kernels):
    count_of_rows, parts_count, length = grid_field.shape
    tile_width = kernels.shape[2]
    mirror_block_list = length // tile_width
    reshaped_field = grid_field.astype(jnp.float32).reshape(count_of_rows, parts_count, mirror_block_list, tile_width)
    padded = jnp.pad(reshaped_field, ((0, 0), (0, 0), (1, 1), (0, 0)))
    running = jnp.zeros((count_of_rows, parts_count, mirror_block_list, tile_width), jnp.float32)
    for offset in range(3):
        running = running + jnp.einsum("rcbk,ckel->rebl", padded[:, :, offset:offset + mirror_block_list], kernels[offset])
    return running.reshape(count_of_rows, parts_count, length)


def to_tiles(field_plane):
    return field_plane.reshape(BAND_TOTAL, BAND_ROWS, MIRROR_BLOCKS, MIRROR_TILE).transpose(0, 2, 1, 3).reshape(BAND_TOTAL * MIRROR_BLOCKS, BAND_ROWS, MIRROR_TILE)


def from_tiles(stacked_tiles):
    return stacked_tiles.reshape(BAND_TOTAL, MIRROR_BLOCKS, BAND_ROWS, MIRROR_TILE).transpose(0, 2, 1, 3).reshape(GRID_CELLS, GRID_CELLS)


def reference(mode_field, figure, target, footprint, approach_tiles, focus_tiles):
    approach = real_kernels(approach_tiles)
    focus = real_kernels(focus_tiles)
    adjoint = jnp.transpose(focus, (0, 3, 4, 1, 2))[::-1]
    flat_index = footprint.reshape(-1).astype(jnp.int32)
    picked = to_tiles(figure.astype(jnp.float32))[flat_index]
    phase_delay = PHASE_FACTOR * from_tiles(picked)
    cosine = jnp.cos(phase_delay)
    sine_part = jnp.sin(phase_delay)

    def forward(power_sum, one_mode):
        propagated = banded(one_mode, approach).astype(jnp.bfloat16)
        turned = jnp.transpose(propagated, (2, 1, 0))
        advanced = banded(turned, approach).astype(jnp.bfloat16)
        real_part = advanced[:, 0].astype(jnp.float32)
        imag_part = advanced[:, 1].astype(jnp.float32)
        screened = jnp.stack([real_part * cosine - imag_part * sine_part, real_part * sine_part + imag_part * cosine], axis=1).astype(jnp.bfloat16)
        detected = banded(screened, focus)
        return power_sum + jnp.sum(detected * detected, axis=1), screened

    intensity, screens = lax.scan(forward, jnp.zeros((GRID_CELLS, GRID_CELLS), jnp.float32), mode_field)
    residual = intensity - target.astype(jnp.float32)

    def backward(sens_sum, screened):
        detected = banded(screened, focus)
        detector_grad = (detected * residual[:, None, :]).astype(jnp.bfloat16)
        mirror_grad = banded(detector_grad, adjoint)
        real_part = screened[:, 0].astype(jnp.float32)
        imag_part = screened[:, 1].astype(jnp.float32)
        return sens_sum + 2.0 * PHASE_FACTOR * (mirror_grad[:, 1] * real_part - mirror_grad[:, 0] * imag_part), None

    beam_sens, _ = lax.scan(backward, jnp.zeros((GRID_CELLS, GRID_CELLS), jnp.float32), screens)
    beam_tiles = to_tiles(beam_sens)
    surface = jnp.zeros_like(beam_tiles).at[flat_index].add(beam_tiles)
    return from_tiles(surface)
```

```python
import functools

import jax
import jax.numpy as jnp
from jax import lax
from jax.experimental import pallas as pl
from jax.experimental.pallas import tpu as pltpu
from jax.sharding import PartitionSpec as P

MIRROR_TILE = 64


PHASE_FACTOR = 4.0


def real_kernels(tile_set):
    real_part = tile_set[:, 0]
    imag_part = tile_set[:, 1]
    upper = jnp.stack([real_part, imag_part], axis=2)
    lower = jnp.stack([-imag_part, real_part], axis=2)
    return jnp.stack([upper, lower], axis=1)


def banded(grid_field, kernels):
    leading = grid_field.shape[:-1]
    tile_width = kernels.shape[2]
    mirror_block_list = grid_field.shape[-1] // tile_width
    reshaped_field = grid_field.reshape(leading + (mirror_block_list, tile_width))
    keep = [(0, 0)] * len(leading)
    centre = jnp.einsum(
        "mrcbk,ckel->mrebl", reshaped_field, kernels[1], preferred_element_type=jnp.float32
    )
    from_lower = jnp.einsum(
        "mrcbk,ckel->mrebl",
        reshaped_field[..., :-1, :],
        kernels[0],
        preferred_element_type=jnp.float32,
    )
    from_upper = jnp.einsum(
        "mrcbk,ckel->mrebl",
        reshaped_field[..., 1:, :],
        kernels[2],
        preferred_element_type=jnp.float32,
    )
    running = (
        centre
        + jnp.pad(from_lower, keep + [(1, 0), (0, 0)])
        + jnp.pad(from_upper, keep + [(0, 1), (0, 0)])
    )
    return running.reshape(grid_field.shape)


def tiles_out(beam_row_lines, receive_hot):
    count_of_rows = beam_row_lines.shape[0]
    reshaped_field = beam_row_lines.reshape(count_of_rows, -1, MIRROR_TILE)
    packed_tiles = jnp.einsum(
        "jsc,rjl->scrl", receive_hot, reshaped_field, precision=lax.Precision.HIGHEST
    )
    return packed_tiles.reshape(
        packed_tiles.shape[0], packed_tiles.shape[1], count_of_rows * MIRROR_TILE
    )


def tiles_in(received_tiles, slot_source):
    reshaped_field = received_tiles.reshape(
        received_tiles.shape[0], received_tiles.shape[1], -1, MIRROR_TILE
    )
    placed = jnp.einsum(
        "dck,dcrl->rkl", slot_source, reshaped_field, precision=lax.Precision.HIGHEST
    )
    return placed.reshape(placed.shape[0], -1)


def fetch_heights(surface_rows, slot_source):
    count_of_bands = slot_source.shape[0]
    subset_rows = surface_rows.shape[0]
    outbound_tiles = jnp.einsum(
        "dck,rkl->dcrl",
        slot_source.astype(jnp.bfloat16),
        surface_rows,
        preferred_element_type=jnp.float32,
    ).astype(jnp.bfloat16)
    outbound_tiles = outbound_tiles.reshape(
        count_of_bands, outbound_tiles.shape[1], subset_rows * MIRROR_TILE
    )
    return outbound_tiles


def general_shards(mode_field, figure, target, footprint, approach_tiles, focus_tiles):
    count_of_bands = lax.axis_size("band")
    band_index = lax.axis_index("band")
    count_of_rows = figure.shape[0]
    mirror_block_list = figure.shape[1] // MIRROR_TILE
    slot_capacity = max(2, 2 * mirror_block_list // count_of_bands)
    approach = real_kernels(approach_tiles)
    focus = real_kernels(focus_tiles)
    adjoint = jnp.transpose(focus, (0, 3, 4, 1, 2))[::-1]
    source_band = footprint // mirror_block_list
    source_block = footprint % mirror_block_list
    column = jnp.arange(mirror_block_list, dtype=jnp.int32)
    earlier = column[None, :] < column[:, None]
    same_band = source_band[:, :, None] == source_band[:, None, :]
    tile_rank = jnp.sum((same_band & earlier[None]).astype(jnp.int32), axis=2)
    slot_ids = jnp.arange(slot_capacity, dtype=jnp.int32)
    band_ids = jnp.arange(count_of_bands, dtype=jnp.int32)
    from_here = (source_band == band_index)[:, None, :] & (
        tile_rank[:, None, :] == slot_ids[None, :, None]
    )
    block_hot = (source_block[:, :, None] == column[None, None, :]).astype(jnp.float32)
    slot_source = jnp.einsum("dcj,djk->dck", from_here.astype(jnp.float32), block_hot)
    my_band = lax.dynamic_index_in_dim(source_band, band_index, 0, keepdims=False)
    my_rank = lax.dynamic_index_in_dim(tile_rank, band_index, 0, keepdims=False)
    receive_hot = (
        (my_band[:, None, None] == band_ids[None, :, None])
        & (my_rank[:, None, None] == slot_ids[None, None, :])
    ).astype(jnp.float32)
    receive_low = receive_hot.astype(jnp.bfloat16)
    surface_owned = figure.reshape(count_of_rows, mirror_block_list, MIRROR_TILE)
    outbound_tiles = fetch_heights(surface_owned, slot_source)
    inbound_tiles = lax.all_to_all(outbound_tiles, "band", split_axis=0, concat_axis=0, tiled=True)
    inbound_tiles = inbound_tiles.reshape(count_of_bands, slot_capacity, count_of_rows, MIRROR_TILE)
    phase_tile_stack = jnp.einsum(
        "jsc,scrl->rjl", receive_low, inbound_tiles, preferred_element_type=jnp.float32
    )
    phase_delay = PHASE_FACTOR * phase_tile_stack.reshape(
        count_of_rows, mirror_block_list * MIRROR_TILE
    )
    cosine = jnp.cos(phase_delay)
    sine_part = jnp.sin(phase_delay)
    propagated = banded(mode_field, approach).astype(jnp.bfloat16)
    moved = lax.all_to_all(propagated, "band", split_axis=3, concat_axis=1, tiled=True)
    turned = jnp.transpose(moved, (0, 3, 2, 1))
    advanced = banded(turned, approach).astype(jnp.bfloat16)
    real_part = advanced[:, :, 0].astype(jnp.float32)
    imag_part = advanced[:, :, 1].astype(jnp.float32)
    screened = jnp.stack(
        [real_part * cosine - imag_part * sine_part, real_part * sine_part + imag_part * cosine],
        axis=2,
    ).astype(jnp.bfloat16)
    detected = banded(screened, focus)
    local_power = jnp.sum(detected * detected, axis=(0, 2))
    intensity = lax.psum(local_power, "mode")
    residual = intensity - target.astype(jnp.float32)
    detector_grad = (detected * residual[None, :, None, :]).astype(jnp.bfloat16)
    mirror_grad = banded(detector_grad, adjoint)
    screen_real = screened[:, :, 0].astype(jnp.float32)
    screen_imag = screened[:, :, 1].astype(jnp.float32)
    local_sens = jnp.sum(
        2.0
        * PHASE_FACTOR
        * (mirror_grad[:, :, 1] * screen_real - mirror_grad[:, :, 0] * screen_imag),
        axis=0,
    )
    beam_share = lax.psum_scatter(local_sens, "mode", scatter_dimension=0, tiled=True)
    returned = lax.all_to_all(
        tiles_out(beam_share, receive_hot), "band", split_axis=0, concat_axis=0, tiled=True
    )
    surface_share = tiles_in(returned, slot_source)
    sensitivity = lax.all_gather(surface_share, "mode", axis=0, tiled=True)
    return sensitivity


VMEM_GRANT = 48 * 1024 * 1024


def half_chunk(data_ref, band, block, to_right):
    start = pl.multiple_of((block // 2) * 128, 128)
    chunk = data_ref[band, :, pl.ds(start, 128)].astype(jnp.float32)
    swapped = (block % 2) != to_right
    return jnp.where(swapped, pltpu.roll(chunk, MIRROR_TILE, 1), chunk)


def gather_kernel(band_ref, block_ref, data_ref, out_ref):
    pairs_each = out_ref.shape[2] // 128
    pairs = out_ref.shape[0] * pairs_each
    rows = out_ref.shape[1]
    left_lanes = lax.broadcasted_iota(jnp.int32, (rows, 128), 1) < MIRROR_TILE

    def one_pair(pair, carry):
        left = half_chunk(data_ref, band_ref[2 * pair], block_ref[2 * pair], 0)
        right = half_chunk(data_ref, band_ref[2 * pair + 1], block_ref[2 * pair + 1], 1)
        start = pl.multiple_of((pair % pairs_each) * 128, 128)
        out_ref[pair // pairs_each, :, pl.ds(start, 128)] = jnp.where(
            left_lanes, left, right
        ).astype(out_ref.dtype)
        return carry

    lax.fori_loop(0, pairs, one_pair, 0, unroll=2)


def gather_tiles(bands, blocks, data, out_shape):
    smem = pl.BlockSpec(memory_space=pltpu.SMEM)
    vmem = pl.BlockSpec(memory_space=pltpu.VMEM)
    return pl.pallas_call(
        gather_kernel,
        out_shape=jax.ShapeDtypeStruct(out_shape, data.dtype),
        in_specs=[smem, smem, vmem],
        out_specs=vmem,
        compiler_params=pltpu.CompilerParams(vmem_limit_bytes=VMEM_GRANT),
        cost_estimate=pl.CostEstimate(flops=0, bytes_accessed=6 << 20, transcendentals=0),
    )(bands, blocks, data)


def collect_kernel(block_ref, valid_ref, data_ref, out_ref):
    out_ref[...] = jnp.zeros_like(out_ref)
    bands, rows, length = data_ref.shape
    slots = length // MIRROR_TILE
    lane_half = lax.broadcasted_iota(jnp.int32, (rows, 128), 1) // MIRROR_TILE

    def one_slot(slot, carry):
        block = block_ref[slot]

        @pl.when(valid_ref[slot] > 0)
        def _():
            tile = half_chunk(data_ref, slot // slots, slot % slots, block % 2)
            start = pl.multiple_of((block // 2) * 128, 128)
            out_ref[:, pl.ds(start, 128)] += jnp.where(lane_half == block % 2, tile, 0.0)

        return carry

    lax.fori_loop(0, bands * slots, one_slot, 0)


def collect_tiles(blocks, valid, data, length):
    smem = pl.BlockSpec(memory_space=pltpu.SMEM)
    vmem = pl.BlockSpec(memory_space=pltpu.VMEM)
    return pl.pallas_call(
        collect_kernel,
        out_shape=jax.ShapeDtypeStruct((data.shape[1], length), jnp.float32),
        in_specs=[smem, smem, vmem],
        out_specs=vmem,
        compiler_params=pltpu.CompilerParams(vmem_limit_bytes=VMEM_GRANT),
        cost_estimate=pl.CostEstimate(flops=0, bytes_accessed=6 << 20, transcendentals=0),
    )(blocks, valid, data)


def approach_kernel(real_ref, imag_ref, weight_ref, out_ref):
    tile = weight_ref.shape[0] // 2
    at = pl.multiple_of(pl.program_id(0) * tile, tile)
    lines = jnp.concatenate(
        [real_ref[:, pl.ds(at, 3 * tile)], imag_ref[:, pl.ds(at, 3 * tile)]], axis=1
    )
    turned = lax.dot_general(
        weight_ref[...], lines, (((1,), (1,)), ((), ())), preferred_element_type=jnp.float32
    ).astype(out_ref.dtype)
    for half in range(lines.shape[0] // tile):
        for part in range(2):
            out_ref[0, :, pl.ds((2 * half + part) * tile, tile)] = turned[
                part * tile : (part + 1) * tile, half * tile : (half + 1) * tile
            ]


def approach_turned(real_lines, imag_lines, weight, modes, bands):
    rows = real_lines.shape[0]
    tile = weight.shape[0] // 2
    tiles = modes * bands
    return pl.pallas_call(
        approach_kernel,
        out_shape=jax.ShapeDtypeStruct((tiles, tile, 2 * rows), jnp.bfloat16),
        grid=(tiles,),
        in_specs=[
            pl.BlockSpec(real_lines.shape, lambda t: (0, 0)),
            pl.BlockSpec(imag_lines.shape, lambda t: (0, 0)),
            pl.BlockSpec(weight.shape, lambda t: (0, 0)),
        ],
        out_specs=pl.BlockSpec(
            (1, tile, 2 * rows), lambda t: ((t % modes) * bands + t // modes, 0, 0)
        ),
        compiler_params=pltpu.CompilerParams(vmem_limit_bytes=VMEM_GRANT),
        cost_estimate=pl.CostEstimate(
            flops=2 * rows * weight.size * tiles, bytes_accessed=8 << 20, transcendentals=0
        ),
    )(real_lines, imag_lines, weight)


def beam_kernel(
    modes, moved_ref, cos_ref, sin_ref, target_ref, approach_ref, focus_ref, adjoint_ref,
    sens_ref, lines, screens, grads, sems,
):
    sources, rows, width = moved_ref.shape
    bands = sources // modes
    tile = focus_ref.shape[1] // 2
    pair = 2 * tile
    tiles = cos_ref.shape[1] // tile

    def fetch(index):
        mode, band = index // bands, index % bands
        return pltpu.make_async_copy(
            moved_ref.at[index],
            lines.at[pl.ds(mode * rows, rows), pl.ds(pair + band * width, width)],
            sems.at[index],
        )

    for index in range(sources):
        fetch(index).start()
    edge = jnp.zeros((lines.shape[0], pair), lines.dtype)
    screens[:, pl.ds(0, pair)] = edge
    screens[:, pl.ds((tiles + 1) * pair, pair)] = edge
    grads[:, pl.ds(0, pair)] = edge
    grads[:, pl.ds((tiles + 1) * pair, pair)] = edge
    lines[:, pl.ds(0, pair)] = edge
    lines[:, pl.ds((tiles + 1) * pair, pair)] = edge
    for index in range(sources):
        fetch(index).wait()

    def window(ref, at):
        return ref[:, pl.ds(pl.multiple_of(at * pair, pair), 3 * pair)]

    def put(ref, at, value):
        ref[:, pl.ds(pl.multiple_of((at + 1) * pair, pair), pair)] = value

    def columns(ref, at):
        return ref[:, pl.ds(pl.multiple_of(at * tile, tile), tile)]

    def product(ref, at, weight_ref):
        return jnp.dot(window(ref, at), weight_ref[...], preferred_element_type=jnp.float32)

    def screen_step(at, carry):
        advanced = product(lines, at, approach_ref).astype(jnp.bfloat16).astype(jnp.float32)
        cosine = jnp.concatenate([columns(cos_ref, at)] * modes, axis=0)
        sine = jnp.concatenate([columns(sin_ref, at)] * modes, axis=0)
        real, imag = advanced[:, :tile], advanced[:, tile:]
        screened = jnp.concatenate(
            [real * cosine - imag * sine, real * sine + imag * cosine], axis=1
        )
        put(screens, at, screened.astype(jnp.bfloat16))
        return carry

    def detect_step(at, carry):
        detected = product(screens, at, focus_ref)
        power = detected * detected
        power = power[:, :tile] + power[:, tile:]
        intensity = power[:rows]
        for mode in range(1, modes):
            intensity = intensity + power[mode * rows : (mode + 1) * rows]
        residual = intensity - columns(target_ref, at).astype(jnp.float32)
        residual = jnp.concatenate([jnp.concatenate([residual] * modes, axis=0)] * 2, axis=1)
        put(grads, at, (detected * residual).astype(jnp.bfloat16))
        return carry

    def sens_step(at, carry):
        grad = product(grads, at, adjoint_ref)
        screened = screens[:, pl.ds(pl.multiple_of((at + 1) * pair, pair), pair)]
        screened = screened.astype(jnp.float32)
        terms = grad[:, tile:] * screened[:, :tile] - grad[:, :tile] * screened[:, tile:]
        sens = terms[:rows]
        for mode in range(1, modes):
            sens = sens + terms[mode * rows : (mode + 1) * rows]
        sens_ref[:, pl.ds(pl.multiple_of(at * tile, tile), tile)] = (
            2.0 * PHASE_FACTOR * sens
        ).astype(sens_ref.dtype)
        return carry

    lax.fori_loop(0, tiles, screen_step, 0, unroll=2)
    lax.fori_loop(0, tiles, detect_step, 0, unroll=2)
    lax.fori_loop(0, tiles, sens_step, 0, unroll=2)


def beam_sensitivity(moved, cosine, sine, target, approach, focus, adjoint, modes):
    rows, length = cosine.shape
    vmem = pl.BlockSpec(memory_space=pltpu.VMEM)
    held = pltpu.VMEM((modes * rows, 2 * length + 2 * focus.shape[1]), jnp.bfloat16)
    return pl.pallas_call(
        functools.partial(beam_kernel, modes),
        out_shape=jax.ShapeDtypeStruct((rows, length), jnp.bfloat16),
        in_specs=[pl.BlockSpec(memory_space=pl.ANY)] + [vmem] * 6,
        out_specs=vmem,
        scratch_shapes=[held, held, held, pltpu.SemaphoreType.DMA((moved.shape[0],))],
        compiler_params=pltpu.CompilerParams(vmem_limit_bytes=VMEM_GRANT),
        cost_estimate=pl.CostEstimate(
            flops=2 * modes * rows * focus.size * (length // (focus.shape[1] // 2)) * 3,
            bytes_accessed=12 << 20,
            transcendentals=0,
        ),
    )(moved, cosine, sine, target, approach, focus, adjoint)


def fast_shards(mode_field, figure, target, footprint, approach_tiles, focus_tiles):
    modes = lax.axis_size("mode")
    bands = lax.axis_size("band")
    mode_index = lax.axis_index("mode")
    band_index = lax.axis_index("band")
    rows, length = figure.shape
    share = rows // modes
    blocks = length // MIRROR_TILE
    slots = max(2, 2 * blocks // bands)
    tile = approach_tiles.shape[-1]

    source_band = footprint // blocks
    source_block = footprint % blocks
    column = jnp.arange(blocks, dtype=jnp.int32)
    same = source_band[:, :, None] == source_band[:, None, :]
    rank = jnp.sum((same & (column[None, :] < column[:, None])[None]).astype(jnp.int32), axis=2)
    slot_ids = jnp.arange(slots, dtype=jnp.int32)
    from_here = (source_band == band_index)[:, None, :] & (
        rank[:, None, :] == slot_ids[None, :, None]
    )
    asked_block = jnp.sum(jnp.where(from_here, source_block[:, None, :], 0), axis=2).reshape(-1)
    asked = jnp.sum(from_here.astype(jnp.int32), axis=2).reshape(-1)
    my_band = lax.dynamic_index_in_dim(source_band, band_index, 0, keepdims=False)
    my_rank = lax.dynamic_index_in_dim(rank, band_index, 0, keepdims=False)
    band_ids = jnp.arange(bands, dtype=jnp.int32)
    mine = (my_band[None, None, :] == band_ids[:, None, None]) & (
        my_rank[None, None, :] == slot_ids[None, :, None]
    )
    back_column = jnp.sum(jnp.where(mine, column[None, None, :], 0), axis=2).reshape(-1)
    no_band = jnp.zeros_like(asked_block)

    packed = (bands, share, slots * MIRROR_TILE)
    heights = lax.dynamic_slice_in_dim(figure, mode_index * share, share, 0)[None]
    outbound = gather_tiles(no_band, asked_block, heights, packed)
    inbound = lax.all_to_all(outbound, "band", split_axis=0, concat_axis=0, tiled=True)

    approach = real_kernels(approach_tiles)
    focus = real_kernels(focus_tiles)
    adjoint = jnp.transpose(focus, (0, 3, 4, 1, 2))[::-1]
    flat = (3 * 2 * tile, 2 * tile)
    turned_weight = jnp.transpose(approach, (3, 4, 1, 0, 2)).reshape(2 * tile, 3 * 2 * tile)
    edges = ((0, 0), (tile, tile))
    real_lines = jnp.pad(mode_field[0, :, 0], edges)
    imag_lines = jnp.pad(mode_field[0, :, 1], edges)
    turned = approach_turned(real_lines, imag_lines, turned_weight, modes, bands)
    moved = lax.all_to_all(turned, ("mode", "band"), split_axis=0, concat_axis=0, tiled=True)

    heights_here = gather_tiles(my_band, my_rank, inbound, (1, share, length))[0]
    phase_delay = PHASE_FACTOR * heights_here.astype(jnp.float32)
    cosine = jnp.cos(phase_delay)
    sine = jnp.sin(phase_delay)
    target_here = lax.dynamic_slice_in_dim(target, mode_index * share, share, 0)

    beam = beam_sensitivity(
        moved, cosine, sine, target_here,
        approach.reshape(flat), focus.reshape(flat), adjoint.reshape(flat), modes,
    )

    back = gather_tiles(no_band, back_column, beam[None], packed)
    returned = lax.all_to_all(back, "band", split_axis=0, concat_axis=0, tiled=True)
    surface = collect_tiles(asked_block, asked, returned, length)

    low = surface.astype(jnp.bfloat16)
    pieces = [surface]
    for step in range(1, modes):
        ring = [(i, (i + step) % modes) for i in range(modes)]
        pieces.append(lax.ppermute(low, "mode", ring).astype(jnp.float32))
    out = []
    for owner in range(modes):
        chosen = pieces[0]
        for step in range(1, modes):
            chosen = jnp.where((mode_index - owner) % modes == step, pieces[step], chosen)
        out.append(chosen)
    return jnp.concatenate(out, axis=0)


def solution(mesh):
    modes, bands = mesh.shape["mode"], mesh.shape["band"]

    def shards(mode_field, figure, target, footprint, approach_tiles, focus_tiles):
        tile = approach_tiles.shape[-1]
        share = figure.shape[0] // modes
        fits = mode_field.shape[0] == 1 and share == tile and figure.shape[0] % tile == 0
        fits = fits and tile == 2 * MIRROR_TILE and figure.shape[1] == modes * bands * tile
        chosen = fast_shards if fits else general_shards
        return chosen(mode_field, figure, target, footprint, approach_tiles, focus_tiles)

    in_specs = (P("mode", "band", None, None), P("band", None), P("band", None), P(), P(), P())
    out_specs = P("band", None)
    return jax.shard_map(shards, mesh=mesh, in_specs=in_specs, out_specs=out_specs, check_vma=False)
```

```python
import functools

import jax
import jax.numpy as jnp
from jax import lax
from jax.experimental import pallas as pl
from jax.experimental.pallas import tpu as pltpu
from jax.sharding import PartitionSpec as P

MIRROR_TILE = 64


PHASE_FACTOR = 4.0


def real_kernels(tile_set):
    real_part = tile_set[:, 0]
    imag_part = tile_set[:, 1]
    upper = jnp.stack([real_part, imag_part], axis=2)
    lower = jnp.stack([-imag_part, real_part], axis=2)
    return jnp.stack([upper, lower], axis=1)


def banded(grid_field, kernels):
    leading = grid_field.shape[:-1]
    tile_width = kernels.shape[2]
    mirror_block_list = grid_field.shape[-1] // tile_width
    reshaped_field = grid_field.reshape(leading + (mirror_block_list, tile_width))
    keep = [(0, 0)] * len(leading)
    centre = jnp.einsum(
        "mrcbk,ckel->mrebl", reshaped_field, kernels[1], preferred_element_type=jnp.float32
    )
    from_lower = jnp.einsum(
        "mrcbk,ckel->mrebl",
        reshaped_field[..., :-1, :],
        kernels[0],
        preferred_element_type=jnp.float32,
    )
    from_upper = jnp.einsum(
        "mrcbk,ckel->mrebl",
        reshaped_field[..., 1:, :],
        kernels[2],
        preferred_element_type=jnp.float32,
    )
    running = (
        centre
        + jnp.pad(from_lower, keep + [(1, 0), (0, 0)])
        + jnp.pad(from_upper, keep + [(0, 1), (0, 0)])
    )
    return running.reshape(grid_field.shape)


def tiles_out(beam_row_lines, receive_hot):
    count_of_rows = beam_row_lines.shape[0]
    reshaped_field = beam_row_lines.reshape(count_of_rows, -1, MIRROR_TILE)
    packed_tiles = jnp.einsum(
        "jsc,rjl->scrl", receive_hot, reshaped_field, precision=lax.Precision.HIGHEST
    )
    return packed_tiles.reshape(
        packed_tiles.shape[0], packed_tiles.shape[1], count_of_rows * MIRROR_TILE
    )


def tiles_in(received_tiles, slot_source):
    reshaped_field = received_tiles.reshape(
        received_tiles.shape[0], received_tiles.shape[1], -1, MIRROR_TILE
    )
    placed = jnp.einsum(
        "dck,dcrl->rkl", slot_source, reshaped_field, precision=lax.Precision.HIGHEST
    )
    return placed.reshape(placed.shape[0], -1)


def fetch_heights(surface_rows, slot_source):
    count_of_bands = slot_source.shape[0]
    subset_rows = surface_rows.shape[0]
    outbound_tiles = jnp.einsum(
        "dck,rkl->dcrl",
        slot_source.astype(jnp.bfloat16),
        surface_rows,
        preferred_element_type=jnp.float32,
    ).astype(jnp.bfloat16)
    outbound_tiles = outbound_tiles.reshape(
        count_of_bands, outbound_tiles.shape[1], subset_rows * MIRROR_TILE
    )
    return outbound_tiles


def general_shards(mode_field, figure, target, footprint, approach_tiles, focus_tiles):
    count_of_bands = lax.axis_size("band")
    band_index = lax.axis_index("band")
    count_of_rows = figure.shape[0]
    mirror_block_list = figure.shape[1] // MIRROR_TILE
    slot_capacity = max(2, 2 * mirror_block_list // count_of_bands)
    approach = real_kernels(approach_tiles)
    focus = real_kernels(focus_tiles)
    adjoint = jnp.transpose(focus, (0, 3, 4, 1, 2))[::-1]
    source_band = footprint // mirror_block_list
    source_block = footprint % mirror_block_list
    column = jnp.arange(mirror_block_list, dtype=jnp.int32)
    earlier = column[None, :] < column[:, None]
    same_band = source_band[:, :, None] == source_band[:, None, :]
    tile_rank = jnp.sum((same_band & earlier[None]).astype(jnp.int32), axis=2)
    slot_ids = jnp.arange(slot_capacity, dtype=jnp.int32)
    band_ids = jnp.arange(count_of_bands, dtype=jnp.int32)
    from_here = (source_band == band_index)[:, None, :] & (
        tile_rank[:, None, :] == slot_ids[None, :, None]
    )
    block_hot = (source_block[:, :, None] == column[None, None, :]).astype(jnp.float32)
    slot_source = jnp.einsum("dcj,djk->dck", from_here.astype(jnp.float32), block_hot)
    my_band = lax.dynamic_index_in_dim(source_band, band_index, 0, keepdims=False)
    my_rank = lax.dynamic_index_in_dim(tile_rank, band_index, 0, keepdims=False)
    receive_hot = (
        (my_band[:, None, None] == band_ids[None, :, None])
        & (my_rank[:, None, None] == slot_ids[None, None, :])
    ).astype(jnp.float32)
    receive_low = receive_hot.astype(jnp.bfloat16)
    surface_owned = figure.reshape(count_of_rows, mirror_block_list, MIRROR_TILE)
    outbound_tiles = fetch_heights(surface_owned, slot_source)
    inbound_tiles = lax.all_to_all(outbound_tiles, "band", split_axis=0, concat_axis=0, tiled=True)
    inbound_tiles = inbound_tiles.reshape(count_of_bands, slot_capacity, count_of_rows, MIRROR_TILE)
    phase_tile_stack = jnp.einsum(
        "jsc,scrl->rjl", receive_low, inbound_tiles, preferred_element_type=jnp.float32
    )
    phase_delay = PHASE_FACTOR * phase_tile_stack.reshape(
        count_of_rows, mirror_block_list * MIRROR_TILE
    )
    cosine = jnp.cos(phase_delay)
    sine_part = jnp.sin(phase_delay)
    propagated = banded(mode_field, approach).astype(jnp.bfloat16)
    moved = lax.all_to_all(propagated, "band", split_axis=3, concat_axis=1, tiled=True)
    turned = jnp.transpose(moved, (0, 3, 2, 1))
    advanced = banded(turned, approach).astype(jnp.bfloat16)
    real_part = advanced[:, :, 0].astype(jnp.float32)
    imag_part = advanced[:, :, 1].astype(jnp.float32)
    screened = jnp.stack(
        [real_part * cosine - imag_part * sine_part, real_part * sine_part + imag_part * cosine],
        axis=2,
    ).astype(jnp.bfloat16)
    detected = banded(screened, focus)
    local_power = jnp.sum(detected * detected, axis=(0, 2))
    intensity = lax.psum(local_power, "mode")
    residual = intensity - target.astype(jnp.float32)
    detector_grad = (detected * residual[None, :, None, :]).astype(jnp.bfloat16)
    mirror_grad = banded(detector_grad, adjoint)
    screen_real = screened[:, :, 0].astype(jnp.float32)
    screen_imag = screened[:, :, 1].astype(jnp.float32)
    local_sens = jnp.sum(
        2.0
        * PHASE_FACTOR
        * (mirror_grad[:, :, 1] * screen_real - mirror_grad[:, :, 0] * screen_imag),
        axis=0,
    )
    beam_share = lax.psum_scatter(local_sens, "mode", scatter_dimension=0, tiled=True)
    returned = lax.all_to_all(
        tiles_out(beam_share, receive_hot), "band", split_axis=0, concat_axis=0, tiled=True
    )
    surface_share = tiles_in(returned, slot_source)
    sensitivity = lax.all_gather(surface_share, "mode", axis=0, tiled=True)
    return sensitivity


VMEM_GRANT = 48 * 1024 * 1024
CHUNKS = 2


def half_chunk(data_ref, band, block, to_right):
    start = pl.multiple_of((block // 2) * 128, 128)
    chunk = data_ref[band, :, pl.ds(start, 128)].astype(jnp.float32)
    swapped = (block % 2) != to_right
    return jnp.where(swapped, pltpu.roll(chunk, MIRROR_TILE, 1), chunk)


def gather_kernel(band_ref, block_ref, data_ref, out_ref):
    pairs_each = out_ref.shape[2] // 128
    pairs = out_ref.shape[0] * pairs_each
    rows = out_ref.shape[1]
    left_lanes = lax.broadcasted_iota(jnp.int32, (rows, 128), 1) < MIRROR_TILE

    def one_pair(pair, carry):
        left = half_chunk(data_ref, band_ref[2 * pair], block_ref[2 * pair], 0)
        right = half_chunk(data_ref, band_ref[2 * pair + 1], block_ref[2 * pair + 1], 1)
        start = pl.multiple_of((pair % pairs_each) * 128, 128)
        out_ref[pair // pairs_each, :, pl.ds(start, 128)] = jnp.where(
            left_lanes, left, right
        ).astype(out_ref.dtype)
        return carry

    lax.fori_loop(0, pairs, one_pair, 0, unroll=2)


def gather_tiles(bands, blocks, data, out_shape):
    smem = pl.BlockSpec(memory_space=pltpu.SMEM)
    vmem = pl.BlockSpec(memory_space=pltpu.VMEM)
    return pl.pallas_call(
        gather_kernel,
        out_shape=jax.ShapeDtypeStruct(out_shape, data.dtype),
        in_specs=[smem, smem, vmem],
        out_specs=vmem,
        compiler_params=pltpu.CompilerParams(vmem_limit_bytes=VMEM_GRANT),
        cost_estimate=pl.CostEstimate(flops=0, bytes_accessed=6 << 20, transcendentals=0),
    )(bands, blocks, data)


def collect_kernel(block_ref, valid_ref, data_ref, out_ref):
    out_ref[...] = jnp.zeros_like(out_ref)
    bands, rows, length = data_ref.shape
    slots = length // MIRROR_TILE
    lane_half = lax.broadcasted_iota(jnp.int32, (rows, 128), 1) // MIRROR_TILE

    def one_slot(slot, carry):
        block = block_ref[slot]

        @pl.when(valid_ref[slot] > 0)
        def _():
            tile = half_chunk(data_ref, slot // slots, slot % slots, block % 2)
            start = pl.multiple_of((block // 2) * 128, 128)
            out_ref[:, pl.ds(start, 128)] += jnp.where(lane_half == block % 2, tile, 0.0)

        return carry

    lax.fori_loop(0, bands * slots, one_slot, 0)


def collect_tiles(blocks, valid, data, length):
    smem = pl.BlockSpec(memory_space=pltpu.SMEM)
    vmem = pl.BlockSpec(memory_space=pltpu.VMEM)
    return pl.pallas_call(
        collect_kernel,
        out_shape=jax.ShapeDtypeStruct((data.shape[1], length), jnp.float32),
        in_specs=[smem, smem, vmem],
        out_specs=vmem,
        compiler_params=pltpu.CompilerParams(vmem_limit_bytes=VMEM_GRANT),
        cost_estimate=pl.CostEstimate(flops=0, bytes_accessed=6 << 20, transcendentals=0),
    )(blocks, valid, data)


def approach_kernel(real_ref, imag_ref, weight_ref, *out_refs):
    tile = weight_ref.shape[0] // 2
    at = pl.multiple_of(pl.program_id(0) * tile, tile)
    lines = jnp.concatenate(
        [real_ref[:, pl.ds(at, 3 * tile)], imag_ref[:, pl.ds(at, 3 * tile)]], axis=1
    )
    turned = lax.dot_general(
        weight_ref[...], lines, (((1,), (1,)), ((), ())), preferred_element_type=jnp.float32
    ).astype(out_refs[0].dtype)
    lines_each = tile // len(out_refs)
    for half in range(lines.shape[0] // tile):
        for part in range(2):
            for chunk, out_ref in enumerate(out_refs):
                first = part * tile + chunk * lines_each
                out_ref[0, :, pl.ds((2 * half + part) * tile, tile)] = turned[
                    first : first + lines_each, half * tile : (half + 1) * tile
                ]


def approach_turned(real_lines, imag_lines, weight, modes, bands):
    rows = real_lines.shape[0]
    tile = weight.shape[0] // 2
    tiles = modes * bands
    return pl.pallas_call(
        approach_kernel,
        out_shape=[jax.ShapeDtypeStruct((tiles, tile // CHUNKS, 2 * rows), jnp.bfloat16)] * CHUNKS,
        grid=(tiles,),
        in_specs=[
            pl.BlockSpec(real_lines.shape, lambda t: (0, 0)),
            pl.BlockSpec(imag_lines.shape, lambda t: (0, 0)),
            pl.BlockSpec(weight.shape, lambda t: (0, 0)),
        ],
        out_specs=[
            pl.BlockSpec(
                (1, tile // CHUNKS, 2 * rows), lambda t: ((t % modes) * bands + t // modes, 0, 0)
            )
        ]
        * CHUNKS,
        compiler_params=pltpu.CompilerParams(vmem_limit_bytes=VMEM_GRANT),
        cost_estimate=pl.CostEstimate(
            flops=2 * rows * weight.size * tiles, bytes_accessed=8 << 20, transcendentals=0
        ),
    )(real_lines, imag_lines, weight)


def beam_kernel(
    modes, moved_ref, cos_ref, sin_ref, target_ref, approach_ref, focus_ref, adjoint_ref,
    sens_ref, lines, screens, grads, sems,
):
    sources, rows, width = moved_ref.shape
    bands = sources // modes
    tile = focus_ref.shape[1] // 2
    pair = 2 * tile
    tiles = cos_ref.shape[1] // tile

    def fetch(index):
        mode, band = index // bands, index % bands
        return pltpu.make_async_copy(
            moved_ref.at[index],
            lines.at[pl.ds(mode * rows, rows), pl.ds(pair + band * width, width)],
            sems.at[index],
        )

    for index in range(sources):
        fetch(index).start()
    edge = jnp.zeros((lines.shape[0], pair), lines.dtype)
    screens[:, pl.ds(0, pair)] = edge
    screens[:, pl.ds((tiles + 1) * pair, pair)] = edge
    grads[:, pl.ds(0, pair)] = edge
    grads[:, pl.ds((tiles + 1) * pair, pair)] = edge
    lines[:, pl.ds(0, pair)] = edge
    lines[:, pl.ds((tiles + 1) * pair, pair)] = edge
    for index in range(sources):
        fetch(index).wait()

    def window(ref, at):
        return ref[:, pl.ds(pl.multiple_of(at * pair, pair), 3 * pair)]

    def put(ref, at, value):
        ref[:, pl.ds(pl.multiple_of((at + 1) * pair, pair), pair)] = value

    def columns(ref, at):
        return ref[:, pl.ds(pl.multiple_of(at * tile, tile), tile)]

    def product(ref, at, weight_ref):
        return jnp.dot(window(ref, at), weight_ref[...], preferred_element_type=jnp.float32)

    def screen_step(at, carry):
        advanced = product(lines, at, approach_ref).astype(jnp.bfloat16).astype(jnp.float32)
        cosine = jnp.concatenate([columns(cos_ref, at)] * modes, axis=0)
        sine = jnp.concatenate([columns(sin_ref, at)] * modes, axis=0)
        real, imag = advanced[:, :tile], advanced[:, tile:]
        screened = jnp.concatenate(
            [real * cosine - imag * sine, real * sine + imag * cosine], axis=1
        )
        put(screens, at, screened.astype(jnp.bfloat16))
        return carry

    def detect_step(at, carry):
        detected = product(screens, at, focus_ref)
        power = detected * detected
        power = power[:, :tile] + power[:, tile:]
        intensity = power[:rows]
        for mode in range(1, modes):
            intensity = intensity + power[mode * rows : (mode + 1) * rows]
        residual = intensity - columns(target_ref, at).astype(jnp.float32)
        residual = jnp.concatenate([jnp.concatenate([residual] * modes, axis=0)] * 2, axis=1)
        put(grads, at, (detected * residual).astype(jnp.bfloat16))
        return carry

    def sens_step(at, carry):
        grad = product(grads, at, adjoint_ref)
        screened = screens[:, pl.ds(pl.multiple_of((at + 1) * pair, pair), pair)]
        screened = screened.astype(jnp.float32)
        terms = grad[:, tile:] * screened[:, :tile] - grad[:, :tile] * screened[:, tile:]
        sens = terms[:rows]
        for mode in range(1, modes):
            sens = sens + terms[mode * rows : (mode + 1) * rows]
        sens_ref[:, pl.ds(pl.multiple_of(at * tile, tile), tile)] = (
            2.0 * PHASE_FACTOR * sens
        ).astype(sens_ref.dtype)
        return carry

    lax.fori_loop(0, tiles, screen_step, 0, unroll=2)
    lax.fori_loop(0, tiles, detect_step, 0, unroll=2)
    lax.fori_loop(0, tiles, sens_step, 0, unroll=2)


def beam_sensitivity(chunk, moved, cosine, sine, target, approach, focus, adjoint, modes):
    rows, length = moved.shape[1], cosine.shape[1]
    part = pl.BlockSpec((rows, length), lambda i: (chunk, 0))
    vmem = pl.BlockSpec(memory_space=pltpu.VMEM)
    held = pltpu.VMEM((modes * rows, 2 * length + 2 * focus.shape[1]), jnp.bfloat16)
    return pl.pallas_call(
        functools.partial(beam_kernel, modes),
        out_shape=jax.ShapeDtypeStruct((rows, length), jnp.bfloat16),
        grid=(1,),
        in_specs=[pl.BlockSpec(memory_space=pl.ANY)] + [part] * 3 + [vmem] * 3,
        out_specs=vmem,
        scratch_shapes=[held, held, held, pltpu.SemaphoreType.DMA((moved.shape[0],))],
        compiler_params=pltpu.CompilerParams(vmem_limit_bytes=VMEM_GRANT),
        cost_estimate=pl.CostEstimate(
            flops=2 * modes * rows * focus.size * (length // (focus.shape[1] // 2)) * 3,
            bytes_accessed=12 << 20,
            transcendentals=0,
        ),
    )(moved, cosine, sine, target, approach, focus, adjoint)


def join_kernel(owner_ref, *refs):
    out_ref = refs[-1]
    steps = owner_ref.shape[0]
    lines = refs[0].shape[0]
    each = (len(refs) - 1) // steps
    for step in range(steps):
        first = owner_ref[step] * (each * lines)
        for chunk in range(each):
            at = pl.multiple_of(first + chunk * lines, lines)
            out_ref[pl.ds(at, lines), :] = refs[step * each + chunk][...].astype(out_ref.dtype)


def join_shares(owners, pieces, rows, length):
    flat = [piece for step in pieces for piece in step]
    vmem = pl.BlockSpec(memory_space=pltpu.VMEM)
    return pl.pallas_call(
        join_kernel,
        out_shape=jax.ShapeDtypeStruct((rows, length), jnp.float32),
        in_specs=[pl.BlockSpec(memory_space=pltpu.SMEM)] + [vmem] * len(flat),
        out_specs=vmem,
        compiler_params=pltpu.CompilerParams(vmem_limit_bytes=VMEM_GRANT),
        cost_estimate=pl.CostEstimate(flops=0, bytes_accessed=8 << 20, transcendentals=0),
    )(owners, *flat)


def fast_shards(mode_field, figure, target, footprint, approach_tiles, focus_tiles):
    modes = lax.axis_size("mode")
    bands = lax.axis_size("band")
    mode_index = lax.axis_index("mode")
    band_index = lax.axis_index("band")
    rows, length = figure.shape
    share = rows // modes
    blocks = length // MIRROR_TILE
    slots = max(2, 2 * blocks // bands)
    tile = approach_tiles.shape[-1]

    source_band = footprint // blocks
    source_block = footprint % blocks
    column = jnp.arange(blocks, dtype=jnp.int32)
    same = source_band[:, :, None] == source_band[:, None, :]
    rank = jnp.sum((same & (column[None, :] < column[:, None])[None]).astype(jnp.int32), axis=2)
    slot_ids = jnp.arange(slots, dtype=jnp.int32)
    from_here = (source_band == band_index)[:, None, :] & (
        rank[:, None, :] == slot_ids[None, :, None]
    )
    asked_block = jnp.sum(jnp.where(from_here, source_block[:, None, :], 0), axis=2).reshape(-1)
    asked = jnp.sum(from_here.astype(jnp.int32), axis=2).reshape(-1)
    my_band = lax.dynamic_index_in_dim(source_band, band_index, 0, keepdims=False)
    my_rank = lax.dynamic_index_in_dim(rank, band_index, 0, keepdims=False)
    band_ids = jnp.arange(bands, dtype=jnp.int32)
    mine = (my_band[None, None, :] == band_ids[:, None, None]) & (
        my_rank[None, None, :] == slot_ids[None, :, None]
    )
    back_column = jnp.sum(jnp.where(mine, column[None, None, :], 0), axis=2).reshape(-1)
    no_band = jnp.zeros_like(asked_block)

    packed = (bands, share, slots * MIRROR_TILE)
    heights = lax.dynamic_slice_in_dim(figure, mode_index * share, share, 0)[None]
    outbound = gather_tiles(no_band, asked_block, heights, packed)
    inbound = lax.all_to_all(outbound, "band", split_axis=0, concat_axis=0, tiled=True)

    approach = real_kernels(approach_tiles)
    focus = real_kernels(focus_tiles)
    adjoint = jnp.transpose(focus, (0, 3, 4, 1, 2))[::-1]
    flat = (3 * 2 * tile, 2 * tile)
    turned_weight = jnp.transpose(approach, (3, 4, 1, 0, 2)).reshape(2 * tile, 3 * 2 * tile)
    edges = ((0, 0), (tile, tile))
    real_lines = jnp.pad(mode_field[0, :, 0], edges)
    imag_lines = jnp.pad(mode_field[0, :, 1], edges)
    turned = approach_turned(real_lines, imag_lines, turned_weight, modes, bands)
    moved = [
        lax.all_to_all(part, ("mode", "band"), split_axis=0, concat_axis=0, tiled=True)
        for part in turned
    ]

    heights_here = gather_tiles(my_band, my_rank, inbound, (1, share, length))[0]
    phase_delay = PHASE_FACTOR * heights_here.astype(jnp.float32)
    cosine = jnp.cos(phase_delay)
    sine = jnp.sin(phase_delay)
    target_here = lax.dynamic_slice_in_dim(target, mode_index * share, share, 0)

    weights = (approach.reshape(flat), focus.reshape(flat), adjoint.reshape(flat))
    packed_part = (bands, share // CHUNKS, slots * MIRROR_TILE)
    pieces = [[] for step in range(modes)]
    for chunk in range(CHUNKS):
        beam = beam_sensitivity(chunk, moved[chunk], cosine, sine, target_here, *weights, modes)
        back = gather_tiles(no_band, back_column, beam[None], packed_part)
        returned = lax.all_to_all(back, "band", split_axis=0, concat_axis=0, tiled=True)
        surface = collect_tiles(asked_block, asked, returned, length)
        pieces[0].append(surface)
        low = surface.astype(jnp.bfloat16)
        for step in range(1, modes):
            ring = [(i, (i + step) % modes) for i in range(modes)]
            pieces[step].append(lax.ppermute(low, "mode", ring))
    owners = jnp.remainder(mode_index - jnp.arange(modes, dtype=jnp.int32), modes)
    return join_shares(owners.astype(jnp.int32), pieces, rows, length)


def solution(mesh):
    modes, bands = mesh.shape["mode"], mesh.shape["band"]

    def shards(mode_field, figure, target, footprint, approach_tiles, focus_tiles):
        tile = approach_tiles.shape[-1]
        share = figure.shape[0] // modes
        fits = mode_field.shape[0] == 1 and share == tile and figure.shape[0] % tile == 0
        fits = fits and tile == 2 * MIRROR_TILE and figure.shape[1] == modes * bands * tile
        chosen = fast_shards if fits else general_shards
        return chosen(mode_field, figure, target, footprint, approach_tiles, focus_tiles)

    in_specs = (P("mode", "band", None, None), P("band", None), P("band", None), P(), P(), P())
    out_specs = P("band", None)
    return jax.shard_map(shards, mesh=mesh, in_specs=in_specs, out_specs=out_specs, check_vma=False)
```

```python
import functools
import math

import jax
import jax.numpy as jnp
from jax import lax
from jax.experimental import pallas as pl
from jax.experimental.pallas import tpu as pltpu
from jax.sharding import PartitionSpec as P

MIRROR_TILE = 64


PHASE_FACTOR = 4.0


def real_kernels(tile_set):
    real_part = tile_set[:, 0]
    imag_part = tile_set[:, 1]
    upper = jnp.stack([real_part, imag_part], axis=2)
    lower = jnp.stack([-imag_part, real_part], axis=2)
    return jnp.stack([upper, lower], axis=1)


def banded(grid_field, kernels):
    leading = grid_field.shape[:-1]
    tile_width = kernels.shape[2]
    mirror_block_list = grid_field.shape[-1] // tile_width
    reshaped_field = grid_field.reshape(leading + (mirror_block_list, tile_width))
    keep = [(0, 0)] * len(leading)
    centre = jnp.einsum(
        "mrcbk,ckel->mrebl", reshaped_field, kernels[1], preferred_element_type=jnp.float32
    )
    from_lower = jnp.einsum(
        "mrcbk,ckel->mrebl",
        reshaped_field[..., :-1, :],
        kernels[0],
        preferred_element_type=jnp.float32,
    )
    from_upper = jnp.einsum(
        "mrcbk,ckel->mrebl",
        reshaped_field[..., 1:, :],
        kernels[2],
        preferred_element_type=jnp.float32,
    )
    running = (
        centre
        + jnp.pad(from_lower, keep + [(1, 0), (0, 0)])
        + jnp.pad(from_upper, keep + [(0, 1), (0, 0)])
    )
    return running.reshape(grid_field.shape)


def tiles_out(beam_row_lines, receive_hot):
    count_of_rows = beam_row_lines.shape[0]
    reshaped_field = beam_row_lines.reshape(count_of_rows, -1, MIRROR_TILE)
    packed_tiles = jnp.einsum(
        "jsc,rjl->scrl", receive_hot, reshaped_field, precision=lax.Precision.HIGHEST
    )
    return packed_tiles.reshape(
        packed_tiles.shape[0], packed_tiles.shape[1], count_of_rows * MIRROR_TILE
    )


def tiles_in(received_tiles, slot_source):
    reshaped_field = received_tiles.reshape(
        received_tiles.shape[0], received_tiles.shape[1], -1, MIRROR_TILE
    )
    placed = jnp.einsum(
        "dck,dcrl->rkl", slot_source, reshaped_field, precision=lax.Precision.HIGHEST
    )
    return placed.reshape(placed.shape[0], -1)


def fetch_heights(surface_rows, slot_source):
    count_of_bands = slot_source.shape[0]
    subset_rows = surface_rows.shape[0]
    outbound_tiles = jnp.einsum(
        "dck,rkl->dcrl",
        slot_source.astype(jnp.bfloat16),
        surface_rows,
        preferred_element_type=jnp.float32,
    ).astype(jnp.bfloat16)
    outbound_tiles = outbound_tiles.reshape(
        count_of_bands, outbound_tiles.shape[1], subset_rows * MIRROR_TILE
    )
    return outbound_tiles


def general_shards(mode_field, figure, target, footprint, approach_tiles, focus_tiles):
    count_of_bands = lax.axis_size("band")
    band_index = lax.axis_index("band")
    count_of_rows = figure.shape[0]
    mirror_block_list = figure.shape[1] // MIRROR_TILE
    slot_capacity = max(2, 2 * mirror_block_list // count_of_bands)
    approach = real_kernels(approach_tiles)
    focus = real_kernels(focus_tiles)
    adjoint = jnp.transpose(focus, (0, 3, 4, 1, 2))[::-1]
    source_band = footprint // mirror_block_list
    source_block = footprint % mirror_block_list
    column = jnp.arange(mirror_block_list, dtype=jnp.int32)
    earlier = column[None, :] < column[:, None]
    same_band = source_band[:, :, None] == source_band[:, None, :]
    tile_rank = jnp.sum((same_band & earlier[None]).astype(jnp.int32), axis=2)
    slot_ids = jnp.arange(slot_capacity, dtype=jnp.int32)
    band_ids = jnp.arange(count_of_bands, dtype=jnp.int32)
    from_here = (source_band == band_index)[:, None, :] & (
        tile_rank[:, None, :] == slot_ids[None, :, None]
    )
    block_hot = (source_block[:, :, None] == column[None, None, :]).astype(jnp.float32)
    slot_source = jnp.einsum("dcj,djk->dck", from_here.astype(jnp.float32), block_hot)
    my_band = lax.dynamic_index_in_dim(source_band, band_index, 0, keepdims=False)
    my_rank = lax.dynamic_index_in_dim(tile_rank, band_index, 0, keepdims=False)
    receive_hot = (
        (my_band[:, None, None] == band_ids[None, :, None])
        & (my_rank[:, None, None] == slot_ids[None, None, :])
    ).astype(jnp.float32)
    receive_low = receive_hot.astype(jnp.bfloat16)
    surface_owned = figure.reshape(count_of_rows, mirror_block_list, MIRROR_TILE)
    outbound_tiles = fetch_heights(surface_owned, slot_source)
    inbound_tiles = lax.all_to_all(outbound_tiles, "band", split_axis=0, concat_axis=0, tiled=True)
    inbound_tiles = inbound_tiles.reshape(count_of_bands, slot_capacity, count_of_rows, MIRROR_TILE)
    phase_tile_stack = jnp.einsum(
        "jsc,scrl->rjl", receive_low, inbound_tiles, preferred_element_type=jnp.float32
    )
    phase_delay = PHASE_FACTOR * phase_tile_stack.reshape(
        count_of_rows, mirror_block_list * MIRROR_TILE
    )
    cosine = jnp.cos(phase_delay)
    sine_part = jnp.sin(phase_delay)
    propagated = banded(mode_field, approach).astype(jnp.bfloat16)
    moved = lax.all_to_all(propagated, "band", split_axis=3, concat_axis=1, tiled=True)
    turned = jnp.transpose(moved, (0, 3, 2, 1))
    advanced = banded(turned, approach).astype(jnp.bfloat16)
    real_part = advanced[:, :, 0].astype(jnp.float32)
    imag_part = advanced[:, :, 1].astype(jnp.float32)
    screened = jnp.stack(
        [real_part * cosine - imag_part * sine_part, real_part * sine_part + imag_part * cosine],
        axis=2,
    ).astype(jnp.bfloat16)
    detected = banded(screened, focus)
    local_power = jnp.sum(detected * detected, axis=(0, 2))
    intensity = lax.psum(local_power, "mode")
    residual = intensity - target.astype(jnp.float32)
    detector_grad = (detected * residual[None, :, None, :]).astype(jnp.bfloat16)
    mirror_grad = banded(detector_grad, adjoint)
    screen_real = screened[:, :, 0].astype(jnp.float32)
    screen_imag = screened[:, :, 1].astype(jnp.float32)
    local_sens = jnp.sum(
        2.0
        * PHASE_FACTOR
        * (mirror_grad[:, :, 1] * screen_real - mirror_grad[:, :, 0] * screen_imag),
        axis=0,
    )
    beam_share = lax.psum_scatter(local_sens, "mode", scatter_dimension=0, tiled=True)
    returned = lax.all_to_all(
        tiles_out(beam_share, receive_hot), "band", split_axis=0, concat_axis=0, tiled=True
    )
    surface_share = tiles_in(returned, slot_source)
    sensitivity = lax.all_gather(surface_share, "mode", axis=0, tiled=True)
    return sensitivity


VMEM_GRANT = 48 * 1024 * 1024
EIGHTHS = (5, 3)


def half_chunk(data_ref, band, block, to_right):
    start = pl.multiple_of((block // 2) * 128, 128)
    chunk = data_ref[band, :, pl.ds(start, 128)].astype(jnp.float32)
    swapped = (block % 2) != to_right
    return jnp.where(swapped, pltpu.roll(chunk, MIRROR_TILE, 1), chunk)


def gather_kernel(band_ref, block_ref, data_ref, out_ref):
    pairs_each = out_ref.shape[2] // 128
    pairs = out_ref.shape[0] * pairs_each
    rows = out_ref.shape[1]
    left_lanes = lax.broadcasted_iota(jnp.int32, (rows, 128), 1) < MIRROR_TILE

    def one_pair(pair, carry):
        left = half_chunk(data_ref, band_ref[2 * pair], block_ref[2 * pair], 0)
        right = half_chunk(data_ref, band_ref[2 * pair + 1], block_ref[2 * pair + 1], 1)
        start = pl.multiple_of((pair % pairs_each) * 128, 128)
        out_ref[pair // pairs_each, :, pl.ds(start, 128)] = jnp.where(
            left_lanes, left, right
        ).astype(out_ref.dtype)
        return carry

    lax.fori_loop(0, pairs, one_pair, 0, unroll=8)


def gather_tiles(bands, blocks, data, out_shape):
    smem = pl.BlockSpec(memory_space=pltpu.SMEM)
    vmem = pl.BlockSpec(memory_space=pltpu.VMEM)
    return pl.pallas_call(
        gather_kernel,
        out_shape=jax.ShapeDtypeStruct(out_shape, data.dtype),
        in_specs=[smem, smem, vmem],
        out_specs=vmem,
        compiler_params=pltpu.CompilerParams(vmem_limit_bytes=VMEM_GRANT),
        cost_estimate=pl.CostEstimate(flops=0, bytes_accessed=6 << 20, transcendentals=0),
    )(bands, blocks, data)


def collect_kernel(block_ref, valid_ref, data_ref, out_ref, low_ref, *totals):
    bands, rows, length = data_ref.shape
    slots = length // MIRROR_TILE
    lane_half = lax.broadcasted_iota(jnp.int32, (rows, 128), 1) // MIRROR_TILE
    for total in totals:
        total[...] = jnp.zeros_like(total)

    def some_slots(step, carry):
        for turn, total in enumerate(totals):
            slot = step * len(totals) + turn
            block = block_ref[slot]
            side = block % 2
            tile = half_chunk(data_ref, slot // slots, slot % slots, side)
            lanes = lane_half == jnp.where(valid_ref[slot] > 0, side, 2)
            start = pl.multiple_of((block // 2) * 128, 128)
            total[:, pl.ds(start, 128)] += jnp.where(lanes, tile, 0.0)
        return carry

    lax.fori_loop(0, bands * slots // len(totals), some_slots, 0, unroll=2)
    surface = totals[0][...]
    for total in totals[1:]:
        surface = surface + total[...]
    out_ref[...] = surface
    low_ref[...] = surface.astype(low_ref.dtype)


def collect_tiles(blocks, valid, data, length):
    smem = pl.BlockSpec(memory_space=pltpu.SMEM)
    vmem = pl.BlockSpec(memory_space=pltpu.VMEM)
    extent = (data.shape[1], length)
    return pl.pallas_call(
        collect_kernel,
        out_shape=[
            jax.ShapeDtypeStruct(extent, jnp.float32),
            jax.ShapeDtypeStruct(extent, jnp.bfloat16),
        ],
        in_specs=[smem, smem, vmem],
        out_specs=[vmem, vmem],
        scratch_shapes=[pltpu.VMEM(extent, jnp.float32)] * 4,
        compiler_params=pltpu.CompilerParams(vmem_limit_bytes=VMEM_GRANT),
        cost_estimate=pl.CostEstimate(flops=0, bytes_accessed=6 << 20, transcendentals=0),
    )(blocks, valid, data)


def approach_kernel(real_ref, imag_ref, weight_ref, *out_refs):
    tile = weight_ref.shape[0] // 2
    at = pl.multiple_of(pl.program_id(0) * tile, tile)
    lines = jnp.concatenate(
        [real_ref[:, pl.ds(at, 3 * tile)], imag_ref[:, pl.ds(at, 3 * tile)]], axis=1
    )
    turned = lax.dot_general(
        weight_ref[...], lines, (((1,), (1,)), ((), ())), preferred_element_type=jnp.float32
    ).astype(out_refs[0].dtype)
    for half in range(lines.shape[0] // tile):
        for part in range(2):
            first = part * tile
            for out_ref in out_refs:
                last = first + out_ref.shape[1]
                out_ref[0, :, pl.ds((2 * half + part) * tile, tile)] = turned[
                    first:last, half * tile : (half + 1) * tile
                ]
                first = last


def approach_turned(real_lines, imag_lines, weight, modes, bands, chunks):
    rows = real_lines.shape[0]
    tile = weight.shape[0] // 2
    tiles = modes * bands
    return pl.pallas_call(
        approach_kernel,
        out_shape=[jax.ShapeDtypeStruct((tiles, each, 2 * rows), jnp.bfloat16) for each in chunks],
        grid=(tiles,),
        in_specs=[
            pl.BlockSpec(real_lines.shape, lambda t: (0, 0)),
            pl.BlockSpec(imag_lines.shape, lambda t: (0, 0)),
            pl.BlockSpec(weight.shape, lambda t: (0, 0)),
        ],
        out_specs=[
            pl.BlockSpec(
                (1, each, 2 * rows), lambda t: ((t % modes) * bands + t // modes, 0, 0)
            )
            for each in chunks
        ],
        compiler_params=pltpu.CompilerParams(vmem_limit_bytes=VMEM_GRANT),
        cost_estimate=pl.CostEstimate(
            flops=2 * rows * weight.size * tiles, bytes_accessed=8 << 20, transcendentals=0
        ),
    )(real_lines, imag_lines, weight)


def beam_kernel(
    modes, first, moved_ref, cos_ref, sin_ref, target_ref, approach_ref, focus_ref, adjoint_ref,
    sens_ref, lines, screens, grads, sems,
):
    sources, rows, width = moved_ref.shape
    bands = sources // modes
    tile = focus_ref.shape[1] // 2
    pair = 2 * tile
    tiles = cos_ref.shape[1] // tile

    def fetch(index):
        mode, band = index // bands, index % bands
        return pltpu.make_async_copy(
            moved_ref.at[index],
            lines.at[pl.ds(mode * rows, rows), pl.ds(pair + band * width, width)],
            sems.at[index],
        )

    for index in range(sources):
        fetch(index).start()
    edge = jnp.zeros((lines.shape[0], pair), lines.dtype)
    screens[:, pl.ds(0, pair)] = edge
    screens[:, pl.ds((tiles + 1) * pair, pair)] = edge
    grads[:, pl.ds(0, pair)] = edge
    grads[:, pl.ds((tiles + 1) * pair, pair)] = edge
    lines[:, pl.ds(0, pair)] = edge
    lines[:, pl.ds((tiles + 1) * pair, pair)] = edge
    for index in range(sources):
        fetch(index).wait()

    def window(ref, at):
        return ref[:, pl.ds(pl.multiple_of(at * pair, pair), 3 * pair)]

    def put(ref, at, value):
        ref[:, pl.ds(pl.multiple_of((at + 1) * pair, pair), pair)] = value

    def columns(ref, at):
        return ref[pl.ds(first, rows), pl.ds(pl.multiple_of(at * tile, tile), tile)]

    def product(ref, at, weight_ref):
        return jnp.dot(window(ref, at), weight_ref[...], preferred_element_type=jnp.float32)

    def screen_step(at, carry):
        advanced = product(lines, at, approach_ref).astype(jnp.bfloat16).astype(jnp.float32)
        cosine = jnp.concatenate([columns(cos_ref, at)] * modes, axis=0)
        sine = jnp.concatenate([columns(sin_ref, at)] * modes, axis=0)
        real, imag = advanced[:, :tile], advanced[:, tile:]
        screened = jnp.concatenate(
            [real * cosine - imag * sine, real * sine + imag * cosine], axis=1
        )
        put(screens, at, screened.astype(jnp.bfloat16))
        return carry

    def detect_step(at, carry):
        detected = product(screens, at, focus_ref)
        power = detected * detected
        power = power[:, :tile] + power[:, tile:]
        intensity = power[:rows]
        for mode in range(1, modes):
            intensity = intensity + power[mode * rows : (mode + 1) * rows]
        residual = intensity - columns(target_ref, at).astype(jnp.float32)
        residual = jnp.concatenate([jnp.concatenate([residual] * modes, axis=0)] * 2, axis=1)
        put(grads, at, (detected * residual).astype(jnp.bfloat16))
        return carry

    def sens_step(at, carry):
        grad = product(grads, at, adjoint_ref)
        screened = screens[:, pl.ds(pl.multiple_of((at + 1) * pair, pair), pair)]
        screened = screened.astype(jnp.float32)
        terms = grad[:, tile:] * screened[:, :tile] - grad[:, :tile] * screened[:, tile:]
        sens = terms[:rows]
        for mode in range(1, modes):
            sens = sens + terms[mode * rows : (mode + 1) * rows]
        sens_ref[:, pl.ds(pl.multiple_of(at * tile, tile), tile)] = (
            2.0 * PHASE_FACTOR * sens
        ).astype(sens_ref.dtype)
        return carry

    lax.fori_loop(0, tiles, screen_step, 0, unroll=4)
    lax.fori_loop(0, tiles, detect_step, 0, unroll=4)
    lax.fori_loop(0, tiles, sens_step, 0, unroll=4)


def beam_sensitivity(first, moved, cosine, sine, target, approach, focus, adjoint, modes):
    rows, length = moved.shape[1], cosine.shape[1]
    vmem = pl.BlockSpec(memory_space=pltpu.VMEM)
    held = pltpu.VMEM((modes * rows, 2 * length + 2 * focus.shape[1]), jnp.bfloat16)
    return pl.pallas_call(
        functools.partial(beam_kernel, modes, first),
        out_shape=jax.ShapeDtypeStruct((rows, length), jnp.bfloat16),
        in_specs=[pl.BlockSpec(memory_space=pl.ANY)] + [vmem] * 6,
        out_specs=vmem,
        scratch_shapes=[held, held, held, pltpu.SemaphoreType.DMA((moved.shape[0],))],
        compiler_params=pltpu.CompilerParams(vmem_limit_bytes=VMEM_GRANT),
        cost_estimate=pl.CostEstimate(
            flops=2 * modes * rows * focus.size * (length // (focus.shape[1] // 2)) * 3,
            bytes_accessed=12 << 20,
            transcendentals=0,
        ),
    )(moved, cosine, sine, target, approach, focus, adjoint)


def join_kernel(owner_ref, *refs):
    out_ref = refs[-1]
    steps = owner_ref.shape[0]
    each = (len(refs) - 1) // steps
    share = out_ref.shape[0] // steps
    unit = math.gcd(*[ref.shape[0] for ref in refs])
    for step in range(steps):
        first = owner_ref[step] * share
        for ref in refs[step * each : (step + 1) * each]:
            lines = ref.shape[0]
            at = pl.multiple_of(first, unit)
            out_ref[pl.ds(at, lines), :] = ref[...].astype(out_ref.dtype)
            first = first + lines


def join_shares(owners, pieces, rows, length):
    flat = [piece for step in pieces for piece in step]
    vmem = pl.BlockSpec(memory_space=pltpu.VMEM)
    return pl.pallas_call(
        join_kernel,
        out_shape=jax.ShapeDtypeStruct((rows, length), jnp.float32),
        in_specs=[pl.BlockSpec(memory_space=pltpu.SMEM)] + [vmem] * len(flat),
        out_specs=vmem,
        compiler_params=pltpu.CompilerParams(vmem_limit_bytes=VMEM_GRANT),
        cost_estimate=pl.CostEstimate(flops=0, bytes_accessed=8 << 20, transcendentals=0),
    )(owners, *flat)


def fast_shards(mode_field, figure, target, footprint, approach_tiles, focus_tiles):
    modes = lax.axis_size("mode")
    bands = lax.axis_size("band")
    mode_index = lax.axis_index("mode")
    band_index = lax.axis_index("band")
    rows, length = figure.shape
    share = rows // modes
    blocks = length // MIRROR_TILE
    slots = max(2, 2 * blocks // bands)
    chunks = [share * eighths // sum(EIGHTHS) for eighths in EIGHTHS]
    tile = approach_tiles.shape[-1]

    source_band = footprint // blocks
    source_block = footprint % blocks
    column = jnp.arange(blocks, dtype=jnp.int32)
    same = source_band[:, :, None] == source_band[:, None, :]
    rank = jnp.sum((same & (column[None, :] < column[:, None])[None]).astype(jnp.int32), axis=2)
    slot_ids = jnp.arange(slots, dtype=jnp.int32)
    from_here = (source_band == band_index)[:, None, :] & (
        rank[:, None, :] == slot_ids[None, :, None]
    )
    asked_block = jnp.sum(jnp.where(from_here, source_block[:, None, :], 0), axis=2).reshape(-1)
    asked = jnp.sum(from_here.astype(jnp.int32), axis=2).reshape(-1)
    my_band = lax.dynamic_index_in_dim(source_band, band_index, 0, keepdims=False)
    my_rank = lax.dynamic_index_in_dim(rank, band_index, 0, keepdims=False)
    band_ids = jnp.arange(bands, dtype=jnp.int32)
    mine = (my_band[None, None, :] == band_ids[:, None, None]) & (
        my_rank[None, None, :] == slot_ids[None, :, None]
    )
    back_column = jnp.sum(jnp.where(mine, column[None, None, :], 0), axis=2).reshape(-1)
    no_band = jnp.zeros_like(asked_block)

    packed = (bands, share, slots * MIRROR_TILE)
    heights = lax.dynamic_slice_in_dim(figure, mode_index * share, share, 0)[None]
    outbound = gather_tiles(no_band, asked_block, heights, packed)
    inbound = lax.all_to_all(outbound, "band", split_axis=0, concat_axis=0, tiled=True)

    approach = real_kernels(approach_tiles)
    focus = real_kernels(focus_tiles)
    adjoint = jnp.transpose(focus, (0, 3, 4, 1, 2))[::-1]
    flat = (3 * 2 * tile, 2 * tile)
    turned_weight = jnp.transpose(approach, (3, 4, 1, 0, 2)).reshape(2 * tile, 3 * 2 * tile)
    edges = ((0, 0), (tile, tile))
    real_lines = jnp.pad(mode_field[0, :, 0], edges)
    imag_lines = jnp.pad(mode_field[0, :, 1], edges)
    turned = approach_turned(real_lines, imag_lines, turned_weight, modes, bands, chunks)
    moved = [
        lax.all_to_all(part, ("mode", "band"), split_axis=0, concat_axis=0, tiled=True)
        for part in turned
    ]

    heights_here = gather_tiles(my_band, my_rank, inbound, (1, share, length))[0]
    phase_delay = PHASE_FACTOR * heights_here.astype(jnp.float32)
    cosine = jnp.cos(phase_delay)
    sine = jnp.sin(phase_delay)
    target_here = lax.dynamic_slice_in_dim(target, mode_index * share, share, 0)

    weights = (approach.reshape(flat), focus.reshape(flat), adjoint.reshape(flat))
    pieces = [[] for step in range(modes)]
    first = 0
    for each, lines in zip(chunks, moved):
        beam = beam_sensitivity(first, lines, cosine, sine, target_here, *weights, modes)
        first += each
        packed_part = (bands, each, slots * MIRROR_TILE)
        back = gather_tiles(no_band, back_column, beam[None], packed_part)
        returned = lax.all_to_all(back, "band", split_axis=0, concat_axis=0, tiled=True)
        surface, low = collect_tiles(asked_block, asked, returned, length)
        pieces[0].append(surface)
        for step in range(1, modes):
            ring = [(i, (i + step) % modes) for i in range(modes)]
            pieces[step].append(lax.ppermute(low, "mode", ring))
    owners = jnp.remainder(mode_index - jnp.arange(modes, dtype=jnp.int32), modes)
    return join_shares(owners.astype(jnp.int32), pieces, rows, length)


def solution(mesh):
    modes, bands = mesh.shape["mode"], mesh.shape["band"]

    def shards(mode_field, figure, target, footprint, approach_tiles, focus_tiles):
        tile = approach_tiles.shape[-1]
        share = figure.shape[0] // modes
        fits = mode_field.shape[0] == 1 and share == tile and figure.shape[0] % tile == 0
        fits = fits and tile == 2 * MIRROR_TILE and figure.shape[1] == modes * bands * tile
        chosen = fast_shards if fits else general_shards
        return chosen(mode_field, figure, target, footprint, approach_tiles, focus_tiles)

    in_specs = (P("mode", "band", None, None), P("band", None), P("band", None), P(), P(), P())
    out_specs = P("band", None)
    return jax.shard_map(shards, mesh=mesh, in_specs=in_specs, out_specs=out_specs, check_vma=False)
```

```python
import functools
import math

import jax
import jax.numpy as jnp
from jax import lax
from jax.experimental import pallas as pl
from jax.experimental.pallas import tpu as pltpu
from jax.sharding import PartitionSpec as P

MIRROR_TILE = 64


PHASE_FACTOR = 4.0


def real_kernels(tile_set):
    real_part = tile_set[:, 0]
    imag_part = tile_set[:, 1]
    upper = jnp.stack([real_part, imag_part], axis=2)
    lower = jnp.stack([-imag_part, real_part], axis=2)
    return jnp.stack([upper, lower], axis=1)


def banded(grid_field, kernels):
    leading = grid_field.shape[:-1]
    tile_width = kernels.shape[2]
    mirror_block_list = grid_field.shape[-1] // tile_width
    reshaped_field = grid_field.reshape(leading + (mirror_block_list, tile_width))
    keep = [(0, 0)] * len(leading)
    centre = jnp.einsum(
        "mrcbk,ckel->mrebl", reshaped_field, kernels[1], preferred_element_type=jnp.float32
    )
    from_lower = jnp.einsum(
        "mrcbk,ckel->mrebl",
        reshaped_field[..., :-1, :],
        kernels[0],
        preferred_element_type=jnp.float32,
    )
    from_upper = jnp.einsum(
        "mrcbk,ckel->mrebl",
        reshaped_field[..., 1:, :],
        kernels[2],
        preferred_element_type=jnp.float32,
    )
    running = (
        centre
        + jnp.pad(from_lower, keep + [(1, 0), (0, 0)])
        + jnp.pad(from_upper, keep + [(0, 1), (0, 0)])
    )
    return running.reshape(grid_field.shape)


def tiles_out(beam_row_lines, receive_hot):
    count_of_rows = beam_row_lines.shape[0]
    reshaped_field = beam_row_lines.reshape(count_of_rows, -1, MIRROR_TILE)
    packed_tiles = jnp.einsum(
        "jsc,rjl->scrl", receive_hot, reshaped_field, precision=lax.Precision.HIGHEST
    )
    return packed_tiles.reshape(
        packed_tiles.shape[0], packed_tiles.shape[1], count_of_rows * MIRROR_TILE
    )


def tiles_in(received_tiles, slot_source):
    reshaped_field = received_tiles.reshape(
        received_tiles.shape[0], received_tiles.shape[1], -1, MIRROR_TILE
    )
    placed = jnp.einsum(
        "dck,dcrl->rkl", slot_source, reshaped_field, precision=lax.Precision.HIGHEST
    )
    return placed.reshape(placed.shape[0], -1)


def fetch_heights(surface_rows, slot_source):
    count_of_bands = slot_source.shape[0]
    subset_rows = surface_rows.shape[0]
    outbound_tiles = jnp.einsum(
        "dck,rkl->dcrl",
        slot_source.astype(jnp.bfloat16),
        surface_rows,
        preferred_element_type=jnp.float32,
    ).astype(jnp.bfloat16)
    outbound_tiles = outbound_tiles.reshape(
        count_of_bands, outbound_tiles.shape[1], subset_rows * MIRROR_TILE
    )
    return outbound_tiles


def general_shards(mode_field, figure, target, footprint, approach_tiles, focus_tiles):
    count_of_bands = lax.axis_size("band")
    band_index = lax.axis_index("band")
    count_of_rows = figure.shape[0]
    mirror_block_list = figure.shape[1] // MIRROR_TILE
    slot_capacity = max(2, 2 * mirror_block_list // count_of_bands)
    approach = real_kernels(approach_tiles)
    focus = real_kernels(focus_tiles)
    adjoint = jnp.transpose(focus, (0, 3, 4, 1, 2))[::-1]
    source_band = footprint // mirror_block_list
    source_block = footprint % mirror_block_list
    column = jnp.arange(mirror_block_list, dtype=jnp.int32)
    earlier = column[None, :] < column[:, None]
    same_band = source_band[:, :, None] == source_band[:, None, :]
    tile_rank = jnp.sum((same_band & earlier[None]).astype(jnp.int32), axis=2)
    slot_ids = jnp.arange(slot_capacity, dtype=jnp.int32)
    band_ids = jnp.arange(count_of_bands, dtype=jnp.int32)
    from_here = (source_band == band_index)[:, None, :] & (
        tile_rank[:, None, :] == slot_ids[None, :, None]
    )
    block_hot = (source_block[:, :, None] == column[None, None, :]).astype(jnp.float32)
    slot_source = jnp.einsum("dcj,djk->dck", from_here.astype(jnp.float32), block_hot)
    my_band = lax.dynamic_index_in_dim(source_band, band_index, 0, keepdims=False)
    my_rank = lax.dynamic_index_in_dim(tile_rank, band_index, 0, keepdims=False)
    receive_hot = (
        (my_band[:, None, None] == band_ids[None, :, None])
        & (my_rank[:, None, None] == slot_ids[None, None, :])
    ).astype(jnp.float32)
    receive_low = receive_hot.astype(jnp.bfloat16)
    surface_owned = figure.reshape(count_of_rows, mirror_block_list, MIRROR_TILE)
    outbound_tiles = fetch_heights(surface_owned, slot_source)
    inbound_tiles = lax.all_to_all(outbound_tiles, "band", split_axis=0, concat_axis=0, tiled=True)
    inbound_tiles = inbound_tiles.reshape(count_of_bands, slot_capacity, count_of_rows, MIRROR_TILE)
    phase_tile_stack = jnp.einsum(
        "jsc,scrl->rjl", receive_low, inbound_tiles, preferred_element_type=jnp.float32
    )
    phase_delay = PHASE_FACTOR * phase_tile_stack.reshape(
        count_of_rows, mirror_block_list * MIRROR_TILE
    )
    cosine = jnp.cos(phase_delay)
    sine_part = jnp.sin(phase_delay)
    propagated = banded(mode_field, approach).astype(jnp.bfloat16)
    moved = lax.all_to_all(propagated, "band", split_axis=3, concat_axis=1, tiled=True)
    turned = jnp.transpose(moved, (0, 3, 2, 1))
    advanced = banded(turned, approach).astype(jnp.bfloat16)
    real_part = advanced[:, :, 0].astype(jnp.float32)
    imag_part = advanced[:, :, 1].astype(jnp.float32)
    screened = jnp.stack(
        [real_part * cosine - imag_part * sine_part, real_part * sine_part + imag_part * cosine],
        axis=2,
    ).astype(jnp.bfloat16)
    detected = banded(screened, focus)
    local_power = jnp.sum(detected * detected, axis=(0, 2))
    intensity = lax.psum(local_power, "mode")
    residual = intensity - target.astype(jnp.float32)
    detector_grad = (detected * residual[None, :, None, :]).astype(jnp.bfloat16)
    mirror_grad = banded(detector_grad, adjoint)
    screen_real = screened[:, :, 0].astype(jnp.float32)
    screen_imag = screened[:, :, 1].astype(jnp.float32)
    local_sens = jnp.sum(
        2.0
        * PHASE_FACTOR
        * (mirror_grad[:, :, 1] * screen_real - mirror_grad[:, :, 0] * screen_imag),
        axis=0,
    )
    beam_share = lax.psum_scatter(local_sens, "mode", scatter_dimension=0, tiled=True)
    returned = lax.all_to_all(
        tiles_out(beam_share, receive_hot), "band", split_axis=0, concat_axis=0, tiled=True
    )
    surface_share = tiles_in(returned, slot_source)
    sensitivity = lax.all_gather(surface_share, "mode", axis=0, tiled=True)
    return sensitivity


VMEM_GRANT = 48 * 1024 * 1024
EIGHTHS = (6, 2)
GROUP = 4


def half_chunk(data_ref, band, block, to_right):
    start = pl.multiple_of((block // 2) * 128, 128)
    chunk = data_ref[band, :, pl.ds(start, 128)].astype(jnp.float32)
    swapped = (block % 2) != to_right
    return jnp.where(swapped, pltpu.roll(chunk, MIRROR_TILE, 1), chunk)


def gather_kernel(band_ref, block_ref, data_ref, out_ref):
    pairs_each = out_ref.shape[2] // 128
    pairs = out_ref.shape[0] * pairs_each
    rows = out_ref.shape[1]
    left_lanes = lax.broadcasted_iota(jnp.int32, (rows, 128), 1) < MIRROR_TILE

    def one_pair(pair, carry):
        left = half_chunk(data_ref, band_ref[2 * pair], block_ref[2 * pair], 0)
        right = half_chunk(data_ref, band_ref[2 * pair + 1], block_ref[2 * pair + 1], 1)
        start = pl.multiple_of((pair % pairs_each) * 128, 128)
        out_ref[pair // pairs_each, :, pl.ds(start, 128)] = jnp.where(
            left_lanes, left, right
        ).astype(out_ref.dtype)
        return carry

    lax.fori_loop(0, pairs, one_pair, 0, unroll=8)


def gather_tiles(bands, blocks, data, out_shape):
    smem = pl.BlockSpec(memory_space=pltpu.SMEM)
    vmem = pl.BlockSpec(memory_space=pltpu.VMEM)
    return pl.pallas_call(
        gather_kernel,
        out_shape=jax.ShapeDtypeStruct(out_shape, data.dtype),
        in_specs=[smem, smem, vmem],
        out_specs=vmem,
        compiler_params=pltpu.CompilerParams(vmem_limit_bytes=VMEM_GRANT),
        cost_estimate=pl.CostEstimate(flops=0, bytes_accessed=6 << 20, transcendentals=0),
    )(bands, blocks, data)


def collect_kernel(block_ref, valid_ref, data_ref, out_ref, low_ref, *totals):
    bands, rows, length = data_ref.shape
    slots = length // MIRROR_TILE
    lane_half = lax.broadcasted_iota(jnp.int32, (rows, 128), 1) // MIRROR_TILE
    for total in totals:
        total[...] = jnp.zeros_like(total)

    def some_slots(step, carry):
        for turn, total in enumerate(totals):
            slot = step * len(totals) + turn
            block = block_ref[slot]
            side = block % 2
            tile = half_chunk(data_ref, slot // slots, slot % slots, side)
            lanes = lane_half == jnp.where(valid_ref[slot] > 0, side, 2)
            start = pl.multiple_of((block // 2) * 128, 128)
            total[:, pl.ds(start, 128)] += jnp.where(lanes, tile, 0.0)
        return carry

    lax.fori_loop(0, bands * slots // len(totals), some_slots, 0, unroll=2)
    surface = totals[0][...]
    for total in totals[1:]:
        surface = surface + total[...]
    out_ref[...] = surface
    low_ref[...] = surface.astype(low_ref.dtype)


def collect_tiles(blocks, valid, data, length):
    smem = pl.BlockSpec(memory_space=pltpu.SMEM)
    vmem = pl.BlockSpec(memory_space=pltpu.VMEM)
    extent = (data.shape[1], length)
    return pl.pallas_call(
        collect_kernel,
        out_shape=[
            jax.ShapeDtypeStruct(extent, jnp.float32),
            jax.ShapeDtypeStruct(extent, jnp.bfloat16),
        ],
        in_specs=[smem, smem, vmem],
        out_specs=[vmem, vmem],
        scratch_shapes=[pltpu.VMEM(extent, jnp.float32)] * 4,
        compiler_params=pltpu.CompilerParams(vmem_limit_bytes=VMEM_GRANT),
        cost_estimate=pl.CostEstimate(flops=0, bytes_accessed=6 << 20, transcendentals=0),
    )(blocks, valid, data)


def approach_kernel(real_ref, imag_ref, weight_ref, *out_refs):
    tile = weight_ref.shape[0] // 2
    at = pl.multiple_of(pl.program_id(0) * tile, tile)
    lines = jnp.concatenate(
        [real_ref[:, pl.ds(at, 3 * tile)], imag_ref[:, pl.ds(at, 3 * tile)]], axis=1
    )
    turned = lax.dot_general(
        weight_ref[...], lines, (((1,), (1,)), ((), ())), preferred_element_type=jnp.float32
    ).astype(out_refs[0].dtype)
    for half in range(lines.shape[0] // tile):
        for part in range(2):
            first = part * tile
            for out_ref in out_refs:
                last = first + out_ref.shape[1]
                out_ref[0, :, pl.ds((2 * half + part) * tile, tile)] = turned[
                    first:last, half * tile : (half + 1) * tile
                ]
                first = last


def approach_turned(real_lines, imag_lines, weight, modes, bands, chunks):
    rows = real_lines.shape[0]
    tile = weight.shape[0] // 2
    tiles = modes * bands
    return pl.pallas_call(
        approach_kernel,
        out_shape=[jax.ShapeDtypeStruct((tiles, each, 2 * rows), jnp.bfloat16) for each in chunks],
        grid=(tiles,),
        in_specs=[
            pl.BlockSpec(real_lines.shape, lambda t: (0, 0)),
            pl.BlockSpec(imag_lines.shape, lambda t: (0, 0)),
            pl.BlockSpec(weight.shape, lambda t: (0, 0)),
        ],
        out_specs=[
            pl.BlockSpec(
                (1, each, 2 * rows), lambda t: ((t % modes) * bands + t // modes, 0, 0)
            )
            for each in chunks
        ],
        compiler_params=pltpu.CompilerParams(vmem_limit_bytes=VMEM_GRANT),
        cost_estimate=pl.CostEstimate(
            flops=2 * rows * weight.size * tiles, bytes_accessed=8 << 20, transcendentals=0
        ),
    )(real_lines, imag_lines, weight)


def beam_kernel(
    modes, first, moved_ref, cos_ref, sin_ref, target_ref, approach_ref, focus_ref, adjoint_ref,
    sens_ref, lines, screens, grads, sems,
):
    sources, rows, width = moved_ref.shape
    bands = sources // modes
    tile = focus_ref.shape[1] // 2
    pair = 2 * tile
    tiles = cos_ref.shape[1] // tile

    def fetch(index):
        mode, band = index // bands, index % bands
        return pltpu.make_async_copy(
            moved_ref.at[index],
            lines.at[pl.ds(mode * rows, rows), pl.ds(pair + band * width, width)],
            sems.at[index],
        )

    for index in range(sources):
        fetch(index).start()
    edge = jnp.zeros((lines.shape[0], pair), lines.dtype)
    screens[:, pl.ds(0, pair)] = edge
    screens[:, pl.ds((tiles + 1) * pair, pair)] = edge
    grads[:, pl.ds(0, pair)] = edge
    grads[:, pl.ds((tiles + 1) * pair, pair)] = edge
    lines[:, pl.ds(0, pair)] = edge
    lines[:, pl.ds((tiles + 1) * pair, pair)] = edge
    for index in range(sources):
        fetch(index).wait()

    def window(ref, at):
        return ref[:, pl.ds(pl.multiple_of(at * pair, pair), 3 * pair)]

    def put(ref, at, value):
        ref[:, pl.ds(pl.multiple_of((at + 1) * pair, pair), pair)] = value

    def columns(ref, at):
        return ref[pl.ds(first, rows), pl.ds(pl.multiple_of(at * tile, tile), tile)]

    group = math.gcd(GROUP, tiles)
    stacked = modes * rows

    def products(ref, first_at, weight_ref):
        windows = jnp.concatenate([window(ref, first_at + turn) for turn in range(group)], axis=0)
        out = jnp.dot(windows, weight_ref[...], preferred_element_type=jnp.float32)
        return [
            (first_at + turn, out[turn * stacked : (turn + 1) * stacked]) for turn in range(group)
        ]

    def mode_sum(value):
        total = value[:rows]
        for mode in range(1, modes):
            total = total + value[mode * rows : (mode + 1) * rows]
        return total

    def screen_step(step, carry):
        for at, advanced in products(lines, step * group, approach_ref):
            advanced = advanced.astype(jnp.bfloat16).astype(jnp.float32)
            cosine = jnp.concatenate([columns(cos_ref, at)] * modes, axis=0)
            sine = jnp.concatenate([columns(sin_ref, at)] * modes, axis=0)
            real, imag = advanced[:, :tile], advanced[:, tile:]
            screened = jnp.concatenate(
                [real * cosine - imag * sine, real * sine + imag * cosine], axis=1
            )
            put(screens, at, screened.astype(jnp.bfloat16))
        return carry

    def detect_step(step, carry):
        for at, detected in products(screens, step * group, focus_ref):
            power = detected * detected
            intensity = mode_sum(power[:, :tile] + power[:, tile:])
            residual = intensity - columns(target_ref, at).astype(jnp.float32)
            residual = jnp.concatenate([residual] * modes, axis=0)
            residual = jnp.concatenate([residual] * 2, axis=1)
            put(grads, at, (detected * residual).astype(jnp.bfloat16))
        return carry

    def sens_step(step, carry):
        for at, grad in products(grads, step * group, adjoint_ref):
            screened = screens[:, pl.ds(pl.multiple_of((at + 1) * pair, pair), pair)]
            screened = screened.astype(jnp.float32)
            terms = grad[:, tile:] * screened[:, :tile] - grad[:, :tile] * screened[:, tile:]
            sens_ref[:, pl.ds(pl.multiple_of(at * tile, tile), tile)] = (
                2.0 * PHASE_FACTOR * mode_sum(terms)
            ).astype(sens_ref.dtype)
        return carry

    lax.fori_loop(0, tiles // group, screen_step, 0)
    lax.fori_loop(0, tiles // group, detect_step, 0)
    lax.fori_loop(0, tiles // group, sens_step, 0)


def beam_sensitivity(first, moved, cosine, sine, target, approach, focus, adjoint, modes):
    rows, length = moved.shape[1], cosine.shape[1]
    vmem = pl.BlockSpec(memory_space=pltpu.VMEM)
    held = pltpu.VMEM((modes * rows, 2 * length + 2 * focus.shape[1]), jnp.bfloat16)
    return pl.pallas_call(
        functools.partial(beam_kernel, modes, first),
        out_shape=jax.ShapeDtypeStruct((rows, length), jnp.bfloat16),
        in_specs=[pl.BlockSpec(memory_space=pl.ANY)] + [vmem] * 6,
        out_specs=vmem,
        scratch_shapes=[held, held, held, pltpu.SemaphoreType.DMA((moved.shape[0],))],
        compiler_params=pltpu.CompilerParams(vmem_limit_bytes=VMEM_GRANT),
        cost_estimate=pl.CostEstimate(
            flops=2 * modes * rows * focus.size * (length // (focus.shape[1] // 2)) * 3,
            bytes_accessed=12 << 20,
            transcendentals=0,
        ),
    )(moved, cosine, sine, target, approach, focus, adjoint)


def join_kernel(owner_ref, *refs):
    out_ref = refs[-1]
    steps = owner_ref.shape[0]
    each = (len(refs) - 1) // steps
    share = out_ref.shape[0] // steps
    unit = math.gcd(*[ref.shape[0] for ref in refs])
    for step in range(steps):
        first = owner_ref[step] * share
        for ref in refs[step * each : (step + 1) * each]:
            lines = ref.shape[0]
            at = pl.multiple_of(first, unit)
            out_ref[pl.ds(at, lines), :] = ref[...].astype(out_ref.dtype)
            first = first + lines


def join_shares(owners, pieces, rows, length):
    flat = [piece for step in pieces for piece in step]
    vmem = pl.BlockSpec(memory_space=pltpu.VMEM)
    return pl.pallas_call(
        join_kernel,
        out_shape=jax.ShapeDtypeStruct((rows, length), jnp.float32),
        in_specs=[pl.BlockSpec(memory_space=pltpu.SMEM)] + [vmem] * len(flat),
        out_specs=vmem,
        compiler_params=pltpu.CompilerParams(vmem_limit_bytes=VMEM_GRANT),
        cost_estimate=pl.CostEstimate(flops=0, bytes_accessed=8 << 20, transcendentals=0),
    )(owners, *flat)


def fast_shards(mode_field, figure, target, footprint, approach_tiles, focus_tiles):
    modes = lax.axis_size("mode")
    bands = lax.axis_size("band")
    mode_index = lax.axis_index("mode")
    band_index = lax.axis_index("band")
    rows, length = figure.shape
    share = rows // modes
    blocks = length // MIRROR_TILE
    slots = max(2, 2 * blocks // bands)
    chunks = [share * eighths // sum(EIGHTHS) for eighths in EIGHTHS]
    tile = approach_tiles.shape[-1]

    source_band = footprint // blocks
    source_block = footprint % blocks
    column = jnp.arange(blocks, dtype=jnp.int32)
    same = source_band[:, :, None] == source_band[:, None, :]
    rank = jnp.sum((same & (column[None, :] < column[:, None])[None]).astype(jnp.int32), axis=2)
    slot_ids = jnp.arange(slots, dtype=jnp.int32)
    from_here = (source_band == band_index)[:, None, :] & (
        rank[:, None, :] == slot_ids[None, :, None]
    )
    asked_block = jnp.sum(jnp.where(from_here, source_block[:, None, :], 0), axis=2).reshape(-1)
    asked = jnp.sum(from_here.astype(jnp.int32), axis=2).reshape(-1)
    my_band = lax.dynamic_index_in_dim(source_band, band_index, 0, keepdims=False)
    my_rank = lax.dynamic_index_in_dim(rank, band_index, 0, keepdims=False)
    band_ids = jnp.arange(bands, dtype=jnp.int32)
    mine = (my_band[None, None, :] == band_ids[:, None, None]) & (
        my_rank[None, None, :] == slot_ids[None, :, None]
    )
    back_column = jnp.sum(jnp.where(mine, column[None, None, :], 0), axis=2).reshape(-1)
    no_band = jnp.zeros_like(asked_block)

    packed = (bands, share, slots * MIRROR_TILE)
    heights = lax.dynamic_slice_in_dim(figure, mode_index * share, share, 0)[None]
    outbound = gather_tiles(no_band, asked_block, heights, packed)
    inbound = lax.all_to_all(outbound, "band", split_axis=0, concat_axis=0, tiled=True)

    approach = real_kernels(approach_tiles)
    focus = real_kernels(focus_tiles)
    adjoint = jnp.transpose(focus, (0, 3, 4, 1, 2))[::-1]
    flat = (3 * 2 * tile, 2 * tile)
    turned_weight = jnp.transpose(approach, (3, 4, 1, 0, 2)).reshape(2 * tile, 3 * 2 * tile)
    edges = ((0, 0), (tile, tile))
    real_lines = jnp.pad(mode_field[0, :, 0], edges)
    imag_lines = jnp.pad(mode_field[0, :, 1], edges)
    turned = approach_turned(real_lines, imag_lines, turned_weight, modes, bands, chunks)
    def to_all(part):
        return lax.all_to_all(part, ("mode", "band"), split_axis=0, concat_axis=0, tiled=True)

    moved = [to_all(turned[0])]

    heights_here = gather_tiles(my_band, my_rank, inbound, (1, share, length))[0]
    phase_delay = PHASE_FACTOR * heights_here.astype(jnp.float32)
    beside = (
        jnp.cos(phase_delay),
        jnp.sin(phase_delay),
        lax.dynamic_slice_in_dim(target, mode_index * share, share, 0),
        approach.reshape(flat),
        focus.reshape(flat),
        adjoint.reshape(flat),
    )
    later, beside = lax.optimization_barrier((turned[1:], beside))
    moved += [to_all(part) for part in later]

    pieces = [[] for step in range(modes)]
    first = 0
    for each, lines in zip(chunks, moved):
        beam = beam_sensitivity(first, lines, *beside, modes)
        first += each
        packed_part = (bands, each, slots * MIRROR_TILE)
        back = gather_tiles(no_band, back_column, beam[None], packed_part)
        returned = lax.all_to_all(back, "band", split_axis=0, concat_axis=0, tiled=True)
        surface, low = collect_tiles(asked_block, asked, returned, length)
        pieces[0].append(surface)
        for step in range(1, modes):
            ring = [(i, (i + step) % modes) for i in range(modes)]
            pieces[step].append(lax.ppermute(low, "mode", ring))
    owners = jnp.remainder(mode_index - jnp.arange(modes, dtype=jnp.int32), modes)
    return join_shares(owners.astype(jnp.int32), pieces, rows, length)


def solution(mesh):
    modes, bands = mesh.shape["mode"], mesh.shape["band"]

    def shards(mode_field, figure, target, footprint, approach_tiles, focus_tiles):
        tile = approach_tiles.shape[-1]
        share = figure.shape[0] // modes
        fits = mode_field.shape[0] == 1 and share == tile and figure.shape[0] % tile == 0
        fits = fits and tile == 2 * MIRROR_TILE and figure.shape[1] == modes * bands * tile
        chosen = fast_shards if fits else general_shards
        return chosen(mode_field, figure, target, footprint, approach_tiles, focus_tiles)

    in_specs = (P("mode", "band", None, None), P("band", None), P("band", None), P(), P(), P())
    out_specs = P("band", None)
    return jax.shard_map(shards, mesh=mesh, in_specs=in_specs, out_specs=out_specs, check_vma=False)
```

```python
import functools
import math

import jax
import jax.numpy as jnp
from jax import lax
from jax.experimental import pallas as pl
from jax.experimental.pallas import tpu as pltpu
from jax.sharding import PartitionSpec as P

MIRROR_TILE = 64


PHASE_FACTOR = 4.0


def real_kernels(tile_set):
    real_part = tile_set[:, 0]
    imag_part = tile_set[:, 1]
    upper = jnp.stack([real_part, imag_part], axis=2)
    lower = jnp.stack([-imag_part, real_part], axis=2)
    return jnp.stack([upper, lower], axis=1)


def banded(grid_field, kernels):
    leading = grid_field.shape[:-1]
    tile_width = kernels.shape[2]
    mirror_block_list = grid_field.shape[-1] // tile_width
    reshaped_field = grid_field.reshape(leading + (mirror_block_list, tile_width))
    keep = [(0, 0)] * len(leading)
    centre = jnp.einsum(
        "mrcbk,ckel->mrebl", reshaped_field, kernels[1], preferred_element_type=jnp.float32
    )
    from_lower = jnp.einsum(
        "mrcbk,ckel->mrebl",
        reshaped_field[..., :-1, :],
        kernels[0],
        preferred_element_type=jnp.float32,
    )
    from_upper = jnp.einsum(
        "mrcbk,ckel->mrebl",
        reshaped_field[..., 1:, :],
        kernels[2],
        preferred_element_type=jnp.float32,
    )
    running = (
        centre
        + jnp.pad(from_lower, keep + [(1, 0), (0, 0)])
        + jnp.pad(from_upper, keep + [(0, 1), (0, 0)])
    )
    return running.reshape(grid_field.shape)


def tiles_out(beam_row_lines, receive_hot):
    count_of_rows = beam_row_lines.shape[0]
    reshaped_field = beam_row_lines.reshape(count_of_rows, -1, MIRROR_TILE)
    packed_tiles = jnp.einsum(
        "jsc,rjl->scrl", receive_hot, reshaped_field, precision=lax.Precision.HIGHEST
    )
    return packed_tiles.reshape(
        packed_tiles.shape[0], packed_tiles.shape[1], count_of_rows * MIRROR_TILE
    )


def tiles_in(received_tiles, slot_source):
    reshaped_field = received_tiles.reshape(
        received_tiles.shape[0], received_tiles.shape[1], -1, MIRROR_TILE
    )
    placed = jnp.einsum(
        "dck,dcrl->rkl", slot_source, reshaped_field, precision=lax.Precision.HIGHEST
    )
    return placed.reshape(placed.shape[0], -1)


def fetch_heights(surface_rows, slot_source):
    count_of_bands = slot_source.shape[0]
    subset_rows = surface_rows.shape[0]
    outbound_tiles = jnp.einsum(
        "dck,rkl->dcrl",
        slot_source.astype(jnp.bfloat16),
        surface_rows,
        preferred_element_type=jnp.float32,
    ).astype(jnp.bfloat16)
    outbound_tiles = outbound_tiles.reshape(
        count_of_bands, outbound_tiles.shape[1], subset_rows * MIRROR_TILE
    )
    return outbound_tiles


def general_shards(mode_field, figure, target, footprint, approach_tiles, focus_tiles):
    count_of_bands = lax.axis_size("band")
    band_index = lax.axis_index("band")
    count_of_rows = figure.shape[0]
    mirror_block_list = figure.shape[1] // MIRROR_TILE
    slot_capacity = max(2, 2 * mirror_block_list // count_of_bands)
    approach = real_kernels(approach_tiles)
    focus = real_kernels(focus_tiles)
    adjoint = jnp.transpose(focus, (0, 3, 4, 1, 2))[::-1]
    source_band = footprint // mirror_block_list
    source_block = footprint % mirror_block_list
    column = jnp.arange(mirror_block_list, dtype=jnp.int32)
    earlier = column[None, :] < column[:, None]
    same_band = source_band[:, :, None] == source_band[:, None, :]
    tile_rank = jnp.sum((same_band & earlier[None]).astype(jnp.int32), axis=2)
    slot_ids = jnp.arange(slot_capacity, dtype=jnp.int32)
    band_ids = jnp.arange(count_of_bands, dtype=jnp.int32)
    from_here = (source_band == band_index)[:, None, :] & (
        tile_rank[:, None, :] == slot_ids[None, :, None]
    )
    block_hot = (source_block[:, :, None] == column[None, None, :]).astype(jnp.float32)
    slot_source = jnp.einsum("dcj,djk->dck", from_here.astype(jnp.float32), block_hot)
    my_band = lax.dynamic_index_in_dim(source_band, band_index, 0, keepdims=False)
    my_rank = lax.dynamic_index_in_dim(tile_rank, band_index, 0, keepdims=False)
    receive_hot = (
        (my_band[:, None, None] == band_ids[None, :, None])
        & (my_rank[:, None, None] == slot_ids[None, None, :])
    ).astype(jnp.float32)
    receive_low = receive_hot.astype(jnp.bfloat16)
    surface_owned = figure.reshape(count_of_rows, mirror_block_list, MIRROR_TILE)
    outbound_tiles = fetch_heights(surface_owned, slot_source)
    inbound_tiles = lax.all_to_all(outbound_tiles, "band", split_axis=0, concat_axis=0, tiled=True)
    inbound_tiles = inbound_tiles.reshape(count_of_bands, slot_capacity, count_of_rows, MIRROR_TILE)
    phase_tile_stack = jnp.einsum(
        "jsc,scrl->rjl", receive_low, inbound_tiles, preferred_element_type=jnp.float32
    )
    phase_delay = PHASE_FACTOR * phase_tile_stack.reshape(
        count_of_rows, mirror_block_list * MIRROR_TILE
    )
    cosine = jnp.cos(phase_delay)
    sine_part = jnp.sin(phase_delay)
    propagated = banded(mode_field, approach).astype(jnp.bfloat16)
    moved = lax.all_to_all(propagated, "band", split_axis=3, concat_axis=1, tiled=True)
    turned = jnp.transpose(moved, (0, 3, 2, 1))
    advanced = banded(turned, approach).astype(jnp.bfloat16)
    real_part = advanced[:, :, 0].astype(jnp.float32)
    imag_part = advanced[:, :, 1].astype(jnp.float32)
    screened = jnp.stack(
        [real_part * cosine - imag_part * sine_part, real_part * sine_part + imag_part * cosine],
        axis=2,
    ).astype(jnp.bfloat16)
    detected = banded(screened, focus)
    local_power = jnp.sum(detected * detected, axis=(0, 2))
    intensity = lax.psum(local_power, "mode")
    residual = intensity - target.astype(jnp.float32)
    detector_grad = (detected * residual[None, :, None, :]).astype(jnp.bfloat16)
    mirror_grad = banded(detector_grad, adjoint)
    screen_real = screened[:, :, 0].astype(jnp.float32)
    screen_imag = screened[:, :, 1].astype(jnp.float32)
    local_sens = jnp.sum(
        2.0
        * PHASE_FACTOR
        * (mirror_grad[:, :, 1] * screen_real - mirror_grad[:, :, 0] * screen_imag),
        axis=0,
    )
    beam_share = lax.psum_scatter(local_sens, "mode", scatter_dimension=0, tiled=True)
    returned = lax.all_to_all(
        tiles_out(beam_share, receive_hot), "band", split_axis=0, concat_axis=0, tiled=True
    )
    surface_share = tiles_in(returned, slot_source)
    sensitivity = lax.all_gather(surface_share, "mode", axis=0, tiled=True)
    return sensitivity


VMEM_GRANT = 48 * 1024 * 1024
EIGHTHS = (5, 3)
GROUP = 4


def half_chunk(data_ref, band, block, to_right):
    start = pl.multiple_of((block // 2) * 128, 128)
    chunk = data_ref[band, :, pl.ds(start, 128)].astype(jnp.float32)
    swapped = (block % 2) != to_right
    return jnp.where(swapped, pltpu.roll(chunk, MIRROR_TILE, 1), chunk)


def gather_kernel(band_ref, block_ref, data_ref, out_ref):
    pairs_each = out_ref.shape[2] // 128
    pairs = out_ref.shape[0] * pairs_each
    rows = out_ref.shape[1]
    left_lanes = lax.broadcasted_iota(jnp.int32, (rows, 128), 1) < MIRROR_TILE

    def one_pair(pair, carry):
        left = half_chunk(data_ref, band_ref[2 * pair], block_ref[2 * pair], 0)
        right = half_chunk(data_ref, band_ref[2 * pair + 1], block_ref[2 * pair + 1], 1)
        start = pl.multiple_of((pair % pairs_each) * 128, 128)
        out_ref[pair // pairs_each, :, pl.ds(start, 128)] = jnp.where(
            left_lanes, left, right
        ).astype(out_ref.dtype)
        return carry

    lax.fori_loop(0, pairs, one_pair, 0, unroll=8)


def gather_tiles(bands, blocks, data, out_shape):
    smem = pl.BlockSpec(memory_space=pltpu.SMEM)
    vmem = pl.BlockSpec(memory_space=pltpu.VMEM)
    return pl.pallas_call(
        gather_kernel,
        out_shape=jax.ShapeDtypeStruct(out_shape, data.dtype),
        in_specs=[smem, smem, vmem],
        out_specs=vmem,
        compiler_params=pltpu.CompilerParams(vmem_limit_bytes=VMEM_GRANT),
        cost_estimate=pl.CostEstimate(flops=0, bytes_accessed=6 << 20, transcendentals=0),
    )(bands, blocks, data)


def collect_kernel(block_ref, valid_ref, data_ref, out_ref, low_ref, *totals):
    bands, rows, length = data_ref.shape
    slots = length // MIRROR_TILE
    lane_half = lax.broadcasted_iota(jnp.int32, (rows, 128), 1) // MIRROR_TILE
    for total in totals:
        total[...] = jnp.zeros_like(total)

    def some_slots(step, carry):
        for turn, total in enumerate(totals):
            slot = step * len(totals) + turn
            block = block_ref[slot]
            side = block % 2
            tile = half_chunk(data_ref, slot // slots, slot % slots, side)
            lanes = lane_half == jnp.where(valid_ref[slot] > 0, side, 2)
            start = pl.multiple_of((block // 2) * 128, 128)
            total[:, pl.ds(start, 128)] += jnp.where(lanes, tile, 0.0)
        return carry

    lax.fori_loop(0, bands * slots // len(totals), some_slots, 0, unroll=4)
    surface = totals[0][...]
    for total in totals[1:]:
        surface = surface + total[...]
    out_ref[...] = surface
    low_ref[...] = surface.astype(low_ref.dtype)


def collect_tiles(blocks, valid, data, length):
    smem = pl.BlockSpec(memory_space=pltpu.SMEM)
    vmem = pl.BlockSpec(memory_space=pltpu.VMEM)
    extent = (data.shape[1], length)
    return pl.pallas_call(
        collect_kernel,
        out_shape=[
            jax.ShapeDtypeStruct(extent, jnp.float32),
            jax.ShapeDtypeStruct(extent, jnp.bfloat16),
        ],
        in_specs=[smem, smem, vmem],
        out_specs=[vmem, vmem],
        scratch_shapes=[pltpu.VMEM(extent, jnp.float32)] * 4,
        compiler_params=pltpu.CompilerParams(vmem_limit_bytes=VMEM_GRANT),
        cost_estimate=pl.CostEstimate(flops=0, bytes_accessed=6 << 20, transcendentals=0),
    )(blocks, valid, data)


def approach_kernel(real_ref, imag_ref, weight_ref, *out_refs):
    tile = weight_ref.shape[0] // 2
    at = pl.multiple_of(pl.program_id(0) * tile, tile)
    lines = jnp.concatenate(
        [real_ref[:, pl.ds(at, 3 * tile)], imag_ref[:, pl.ds(at, 3 * tile)]], axis=1
    )
    turned = lax.dot_general(
        weight_ref[...], lines, (((1,), (1,)), ((), ())), preferred_element_type=jnp.float32
    ).astype(out_refs[0].dtype)
    for half in range(lines.shape[0] // tile):
        for part in range(2):
            first = part * tile
            for out_ref in out_refs:
                last = first + out_ref.shape[1]
                out_ref[0, :, pl.ds((2 * half + part) * tile, tile)] = turned[
                    first:last, half * tile : (half + 1) * tile
                ]
                first = last


def approach_turned(real_lines, imag_lines, weight, modes, bands, chunks):
    rows = real_lines.shape[0]
    tile = weight.shape[0] // 2
    tiles = modes * bands
    return pl.pallas_call(
        approach_kernel,
        out_shape=[jax.ShapeDtypeStruct((tiles, each, 2 * rows), jnp.bfloat16) for each in chunks],
        grid=(tiles,),
        in_specs=[
            pl.BlockSpec(real_lines.shape, lambda t: (0, 0)),
            pl.BlockSpec(imag_lines.shape, lambda t: (0, 0)),
            pl.BlockSpec(weight.shape, lambda t: (0, 0)),
        ],
        out_specs=[
            pl.BlockSpec(
                (1, each, 2 * rows), lambda t: ((t % modes) * bands + t // modes, 0, 0)
            )
            for each in chunks
        ],
        compiler_params=pltpu.CompilerParams(vmem_limit_bytes=VMEM_GRANT),
        cost_estimate=pl.CostEstimate(
            flops=2 * rows * weight.size * tiles, bytes_accessed=8 << 20, transcendentals=0
        ),
    )(real_lines, imag_lines, weight)


def beam_kernel(
    modes, first, moved_ref, cos_ref, sin_ref, target_ref, approach_ref, focus_ref, adjoint_ref,
    sens_ref, lines, screens, grads, sems,
):
    sources, rows, width = moved_ref.shape
    bands = sources // modes
    tile = focus_ref.shape[1] // 2
    pair = 2 * tile
    tiles = cos_ref.shape[1] // tile

    def fetch(index):
        mode, band = index // bands, index % bands
        return pltpu.make_async_copy(
            moved_ref.at[index],
            lines.at[pl.ds(mode * rows, rows), pl.ds(pair + band * width, width)],
            sems.at[index],
        )

    for index in range(sources):
        fetch(index).start()
    edge = jnp.zeros((lines.shape[0], pair), lines.dtype)
    screens[:, pl.ds(0, pair)] = edge
    screens[:, pl.ds((tiles + 1) * pair, pair)] = edge
    grads[:, pl.ds(0, pair)] = edge
    grads[:, pl.ds((tiles + 1) * pair, pair)] = edge
    lines[:, pl.ds(0, pair)] = edge
    lines[:, pl.ds((tiles + 1) * pair, pair)] = edge
    for index in range(sources):
        fetch(index).wait()

    def window(ref, at):
        return ref[:, pl.ds(pl.multiple_of(at * pair, pair), 3 * pair)]

    def put(ref, at, value):
        ref[:, pl.ds(pl.multiple_of((at + 1) * pair, pair), pair)] = value

    def columns(ref, at):
        return ref[pl.ds(first, rows), pl.ds(pl.multiple_of(at * tile, tile), tile)]

    group = math.gcd(GROUP, tiles)
    stacked = modes * rows

    def products(ref, first_at, weight_ref):
        windows = jnp.concatenate([window(ref, first_at + turn) for turn in range(group)], axis=0)
        out = jnp.dot(windows, weight_ref[...], preferred_element_type=jnp.float32)
        return [
            (first_at + turn, out[turn * stacked : (turn + 1) * stacked]) for turn in range(group)
        ]

    def mode_sum(value):
        total = value[:rows]
        for mode in range(1, modes):
            total = total + value[mode * rows : (mode + 1) * rows]
        return total

    def screen_step(step, carry):
        for at, advanced in products(lines, step * group, approach_ref):
            advanced = advanced.astype(jnp.bfloat16).astype(jnp.float32)
            cosine = jnp.concatenate([columns(cos_ref, at)] * modes, axis=0)
            sine = jnp.concatenate([columns(sin_ref, at)] * modes, axis=0)
            real, imag = advanced[:, :tile], advanced[:, tile:]
            screened = jnp.concatenate(
                [real * cosine - imag * sine, real * sine + imag * cosine], axis=1
            )
            put(screens, at, screened.astype(jnp.bfloat16))
        return carry

    def detect_step(step, carry):
        for at, detected in products(screens, step * group, focus_ref):
            power = detected * detected
            intensity = mode_sum(power[:, :tile] + power[:, tile:])
            residual = intensity - columns(target_ref, at).astype(jnp.float32)
            residual = jnp.concatenate([residual] * modes, axis=0)
            residual = jnp.concatenate([residual] * 2, axis=1)
            put(grads, at, (detected * residual).astype(jnp.bfloat16))
        return carry

    def sens_step(step, carry):
        for at, grad in products(grads, step * group, adjoint_ref):
            screened = screens[:, pl.ds(pl.multiple_of((at + 1) * pair, pair), pair)]
            screened = screened.astype(jnp.float32)
            terms = grad[:, tile:] * screened[:, :tile] - grad[:, :tile] * screened[:, tile:]
            sens_ref[:, pl.ds(pl.multiple_of(at * tile, tile), tile)] = (
                2.0 * PHASE_FACTOR * mode_sum(terms)
            ).astype(sens_ref.dtype)
        return carry

    lax.fori_loop(0, tiles // group, screen_step, 0)
    lax.fori_loop(0, tiles // group, detect_step, 0)
    lax.fori_loop(0, tiles // group, sens_step, 0)


def beam_sensitivity(first, moved, cosine, sine, target, approach, focus, adjoint, modes):
    rows, length = moved.shape[1], cosine.shape[1]
    vmem = pl.BlockSpec(memory_space=pltpu.VMEM)
    held = pltpu.VMEM((modes * rows, 2 * length + 2 * focus.shape[1]), jnp.bfloat16)
    return pl.pallas_call(
        functools.partial(beam_kernel, modes, first),
        out_shape=jax.ShapeDtypeStruct((rows, length), jnp.bfloat16),
        in_specs=[pl.BlockSpec(memory_space=pl.ANY)] + [vmem] * 6,
        out_specs=vmem,
        scratch_shapes=[held, held, held, pltpu.SemaphoreType.DMA((moved.shape[0],))],
        compiler_params=pltpu.CompilerParams(vmem_limit_bytes=VMEM_GRANT),
        cost_estimate=pl.CostEstimate(
            flops=2 * modes * rows * focus.size * (length // (focus.shape[1] // 2)) * 3,
            bytes_accessed=12 << 20,
            transcendentals=0,
        ),
    )(moved, cosine, sine, target, approach, focus, adjoint)


def join_kernel(counts, owner_ref, *refs):
    out_ref = refs[-1]
    steps = owner_ref.shape[0]
    share = out_ref.shape[0] // steps
    unit = math.gcd(*[ref.shape[0] for ref in refs])
    position = 0
    for step in range(steps):
        first = owner_ref[step] * share
        for ref in refs[position : position + counts[step]]:
            lines = ref.shape[0]
            at = pl.multiple_of(first, unit)
            out_ref[pl.ds(at, lines), :] = ref[...].astype(out_ref.dtype)
            first = first + lines
        position += counts[step]


def join_shares(owners, pieces, rows, length):
    early = [pieces[0]] + [others[:-1] for others in pieces[1:]]
    flat = [piece for step in early for piece in step]
    vmem = pl.BlockSpec(memory_space=pltpu.VMEM)
    joined = pl.pallas_call(
        functools.partial(join_kernel, [len(step) for step in early]),
        out_shape=jax.ShapeDtypeStruct((rows, length), jnp.float32),
        in_specs=[pl.BlockSpec(memory_space=pltpu.SMEM)] + [vmem] * len(flat),
        out_specs=vmem,
        compiler_params=pltpu.CompilerParams(vmem_limit_bytes=VMEM_GRANT),
        cost_estimate=pl.CostEstimate(flops=0, bytes_accessed=8 << 20, transcendentals=0),
    )(owners, *flat)
    share = rows // len(pieces)
    for step in range(1, len(pieces)):
        last = pieces[step][-1].astype(jnp.float32)
        first = (owners[step] + 1) * share - last.shape[0]
        joined = lax.dynamic_update_slice_in_dim(joined, last, first, 0)
    return joined


def fast_shards(mode_field, figure, target, footprint, approach_tiles, focus_tiles):
    modes = lax.axis_size("mode")
    bands = lax.axis_size("band")
    mode_index = lax.axis_index("mode")
    band_index = lax.axis_index("band")
    rows, length = figure.shape
    share = rows // modes
    blocks = length // MIRROR_TILE
    slots = max(2, 2 * blocks // bands)
    chunks = [share * eighths // sum(EIGHTHS) for eighths in EIGHTHS]
    tile = approach_tiles.shape[-1]

    source_band = footprint // blocks
    source_block = footprint % blocks
    column = jnp.arange(blocks, dtype=jnp.int32)
    same = source_band[:, :, None] == source_band[:, None, :]
    rank = jnp.sum((same & (column[None, :] < column[:, None])[None]).astype(jnp.int32), axis=2)
    slot_ids = jnp.arange(slots, dtype=jnp.int32)
    from_here = (source_band == band_index)[:, None, :] & (
        rank[:, None, :] == slot_ids[None, :, None]
    )
    asked_block = jnp.sum(jnp.where(from_here, source_block[:, None, :], 0), axis=2).reshape(-1)
    asked = jnp.sum(from_here.astype(jnp.int32), axis=2).reshape(-1)
    my_band = lax.dynamic_index_in_dim(source_band, band_index, 0, keepdims=False)
    my_rank = lax.dynamic_index_in_dim(rank, band_index, 0, keepdims=False)
    band_ids = jnp.arange(bands, dtype=jnp.int32)
    mine = (my_band[None, None, :] == band_ids[:, None, None]) & (
        my_rank[None, None, :] == slot_ids[None, :, None]
    )
    back_column = jnp.sum(jnp.where(mine, column[None, None, :], 0), axis=2).reshape(-1)
    no_band = jnp.zeros_like(asked_block)

    packed = (bands, share, slots * MIRROR_TILE)
    heights = lax.dynamic_slice_in_dim(figure, mode_index * share, share, 0)[None]
    outbound = gather_tiles(no_band, asked_block, heights, packed)
    inbound = lax.all_to_all(outbound, "band", split_axis=0, concat_axis=0, tiled=True)

    approach = real_kernels(approach_tiles)
    focus = real_kernels(focus_tiles)
    adjoint = jnp.transpose(focus, (0, 3, 4, 1, 2))[::-1]
    flat = (3 * 2 * tile, 2 * tile)
    turned_weight = jnp.transpose(approach, (3, 4, 1, 0, 2)).reshape(2 * tile, 3 * 2 * tile)
    edges = ((0, 0), (tile, tile))
    real_lines = jnp.pad(mode_field[0, :, 0], edges)
    imag_lines = jnp.pad(mode_field[0, :, 1], edges)
    turned = approach_turned(real_lines, imag_lines, turned_weight, modes, bands, chunks)
    def to_all(part):
        return lax.all_to_all(part, ("mode", "band"), split_axis=0, concat_axis=0, tiled=True)

    moved = [to_all(turned[0])]

    heights_here = gather_tiles(my_band, my_rank, inbound, (1, share, length))[0]
    phase_delay = PHASE_FACTOR * heights_here.astype(jnp.float32)
    beside = (
        jnp.cos(phase_delay),
        jnp.sin(phase_delay),
        lax.dynamic_slice_in_dim(target, mode_index * share, share, 0),
        approach.reshape(flat),
        focus.reshape(flat),
        adjoint.reshape(flat),
    )
    later, beside = lax.optimization_barrier((turned[1:], beside))
    moved += [to_all(part) for part in later]

    pieces = [[] for step in range(modes)]
    first = 0
    for each, lines in zip(chunks, moved):
        beam = beam_sensitivity(first, lines, *beside, modes)
        first += each
        packed_part = (bands, each, slots * MIRROR_TILE)
        back = gather_tiles(no_band, back_column, beam[None], packed_part)
        returned = lax.all_to_all(back, "band", split_axis=0, concat_axis=0, tiled=True)
        surface, low = collect_tiles(asked_block, asked, returned, length)
        pieces[0].append(surface)
        for step in range(1, modes):
            ring = [(i, (i + step) % modes) for i in range(modes)]
            pieces[step].append(lax.ppermute(low, "mode", ring))
    owners = jnp.remainder(mode_index - jnp.arange(modes, dtype=jnp.int32), modes)
    return join_shares(owners.astype(jnp.int32), pieces, rows, length)


def solution(mesh):
    modes, bands = mesh.shape["mode"], mesh.shape["band"]

    def shards(mode_field, figure, target, footprint, approach_tiles, focus_tiles):
        tile = approach_tiles.shape[-1]
        share = figure.shape[0] // modes
        fits = mode_field.shape[0] == 1 and share == tile and figure.shape[0] % tile == 0
        fits = fits and tile == 2 * MIRROR_TILE and figure.shape[1] == modes * bands * tile
        chosen = fast_shards if fits else general_shards
        return chosen(mode_field, figure, target, footprint, approach_tiles, focus_tiles)

    in_specs = (P("mode", "band", None, None), P("band", None), P("band", None), P(), P(), P())
    out_specs = P("band", None)
    return jax.shard_map(shards, mesh=mesh, in_specs=in_specs, out_specs=out_specs, check_vma=False)
```

```python
import functools
import math

import jax
import jax.numpy as jnp
from jax import lax
from jax.experimental import pallas as pl
from jax.experimental.pallas import tpu as pltpu
from jax.sharding import PartitionSpec as P

MIRROR_TILE = 64


PHASE_FACTOR = 4.0


def real_kernels(tile_set):
    real_part = tile_set[:, 0]
    imag_part = tile_set[:, 1]
    upper = jnp.stack([real_part, imag_part], axis=2)
    lower = jnp.stack([-imag_part, real_part], axis=2)
    return jnp.stack([upper, lower], axis=1)


def banded(grid_field, kernels):
    leading = grid_field.shape[:-1]
    tile_width = kernels.shape[2]
    mirror_block_list = grid_field.shape[-1] // tile_width
    reshaped_field = grid_field.reshape(leading + (mirror_block_list, tile_width))
    keep = [(0, 0)] * len(leading)
    centre = jnp.einsum(
        "mrcbk,ckel->mrebl", reshaped_field, kernels[1], preferred_element_type=jnp.float32
    )
    from_lower = jnp.einsum(
        "mrcbk,ckel->mrebl",
        reshaped_field[..., :-1, :],
        kernels[0],
        preferred_element_type=jnp.float32,
    )
    from_upper = jnp.einsum(
        "mrcbk,ckel->mrebl",
        reshaped_field[..., 1:, :],
        kernels[2],
        preferred_element_type=jnp.float32,
    )
    running = (
        centre
        + jnp.pad(from_lower, keep + [(1, 0), (0, 0)])
        + jnp.pad(from_upper, keep + [(0, 1), (0, 0)])
    )
    return running.reshape(grid_field.shape)


def tiles_out(beam_row_lines, receive_hot):
    count_of_rows = beam_row_lines.shape[0]
    reshaped_field = beam_row_lines.reshape(count_of_rows, -1, MIRROR_TILE)
    packed_tiles = jnp.einsum(
        "jsc,rjl->scrl", receive_hot, reshaped_field, precision=lax.Precision.HIGHEST
    )
    return packed_tiles.reshape(
        packed_tiles.shape[0], packed_tiles.shape[1], count_of_rows * MIRROR_TILE
    )


def tiles_in(received_tiles, slot_source):
    reshaped_field = received_tiles.reshape(
        received_tiles.shape[0], received_tiles.shape[1], -1, MIRROR_TILE
    )
    placed = jnp.einsum(
        "dck,dcrl->rkl", slot_source, reshaped_field, precision=lax.Precision.HIGHEST
    )
    return placed.reshape(placed.shape[0], -1)


def fetch_heights(surface_rows, slot_source):
    count_of_bands = slot_source.shape[0]
    subset_rows = surface_rows.shape[0]
    outbound_tiles = jnp.einsum(
        "dck,rkl->dcrl",
        slot_source.astype(jnp.bfloat16),
        surface_rows,
        preferred_element_type=jnp.float32,
    ).astype(jnp.bfloat16)
    outbound_tiles = outbound_tiles.reshape(
        count_of_bands, outbound_tiles.shape[1], subset_rows * MIRROR_TILE
    )
    return outbound_tiles


def general_shards(mode_field, figure, target, footprint, approach_tiles, focus_tiles):
    count_of_bands = lax.axis_size("band")
    band_index = lax.axis_index("band")
    count_of_rows = figure.shape[0]
    mirror_block_list = figure.shape[1] // MIRROR_TILE
    slot_capacity = max(2, 2 * mirror_block_list // count_of_bands)
    approach = real_kernels(approach_tiles)
    focus = real_kernels(focus_tiles)
    adjoint = jnp.transpose(focus, (0, 3, 4, 1, 2))[::-1]
    source_band = footprint // mirror_block_list
    source_block = footprint % mirror_block_list
    column = jnp.arange(mirror_block_list, dtype=jnp.int32)
    earlier = column[None, :] < column[:, None]
    same_band = source_band[:, :, None] == source_band[:, None, :]
    tile_rank = jnp.sum((same_band & earlier[None]).astype(jnp.int32), axis=2)
    slot_ids = jnp.arange(slot_capacity, dtype=jnp.int32)
    band_ids = jnp.arange(count_of_bands, dtype=jnp.int32)
    from_here = (source_band == band_index)[:, None, :] & (
        tile_rank[:, None, :] == slot_ids[None, :, None]
    )
    block_hot = (source_block[:, :, None] == column[None, None, :]).astype(jnp.float32)
    slot_source = jnp.einsum("dcj,djk->dck", from_here.astype(jnp.float32), block_hot)
    my_band = lax.dynamic_index_in_dim(source_band, band_index, 0, keepdims=False)
    my_rank = lax.dynamic_index_in_dim(tile_rank, band_index, 0, keepdims=False)
    receive_hot = (
        (my_band[:, None, None] == band_ids[None, :, None])
        & (my_rank[:, None, None] == slot_ids[None, None, :])
    ).astype(jnp.float32)
    receive_low = receive_hot.astype(jnp.bfloat16)
    surface_owned = figure.reshape(count_of_rows, mirror_block_list, MIRROR_TILE)
    outbound_tiles = fetch_heights(surface_owned, slot_source)
    inbound_tiles = lax.all_to_all(outbound_tiles, "band", split_axis=0, concat_axis=0, tiled=True)
    inbound_tiles = inbound_tiles.reshape(count_of_bands, slot_capacity, count_of_rows, MIRROR_TILE)
    phase_tile_stack = jnp.einsum(
        "jsc,scrl->rjl", receive_low, inbound_tiles, preferred_element_type=jnp.float32
    )
    phase_delay = PHASE_FACTOR * phase_tile_stack.reshape(
        count_of_rows, mirror_block_list * MIRROR_TILE
    )
    cosine = jnp.cos(phase_delay)
    sine_part = jnp.sin(phase_delay)
    propagated = banded(mode_field, approach).astype(jnp.bfloat16)
    moved = lax.all_to_all(propagated, "band", split_axis=3, concat_axis=1, tiled=True)
    turned = jnp.transpose(moved, (0, 3, 2, 1))
    advanced = banded(turned, approach).astype(jnp.bfloat16)
    real_part = advanced[:, :, 0].astype(jnp.float32)
    imag_part = advanced[:, :, 1].astype(jnp.float32)
    screened = jnp.stack(
        [real_part * cosine - imag_part * sine_part, real_part * sine_part + imag_part * cosine],
        axis=2,
    ).astype(jnp.bfloat16)
    detected = banded(screened, focus)
    local_power = jnp.sum(detected * detected, axis=(0, 2))
    intensity = lax.psum(local_power, "mode")
    residual = intensity - target.astype(jnp.float32)
    detector_grad = (detected * residual[None, :, None, :]).astype(jnp.bfloat16)
    mirror_grad = banded(detector_grad, adjoint)
    screen_real = screened[:, :, 0].astype(jnp.float32)
    screen_imag = screened[:, :, 1].astype(jnp.float32)
    local_sens = jnp.sum(
        2.0
        * PHASE_FACTOR
        * (mirror_grad[:, :, 1] * screen_real - mirror_grad[:, :, 0] * screen_imag),
        axis=0,
    )
    beam_share = lax.psum_scatter(local_sens, "mode", scatter_dimension=0, tiled=True)
    returned = lax.all_to_all(
        tiles_out(beam_share, receive_hot), "band", split_axis=0, concat_axis=0, tiled=True
    )
    surface_share = tiles_in(returned, slot_source)
    sensitivity = lax.all_gather(surface_share, "mode", axis=0, tiled=True)
    return sensitivity


VMEM_GRANT = 48 * 1024 * 1024
EIGHTHS = (5, 3)
GROUP = 4


def half_chunk(data_ref, band, block, to_right):
    start = pl.multiple_of((block // 2) * 128, 128)
    chunk = data_ref[band, :, pl.ds(start, 128)].astype(jnp.float32)
    swapped = (block % 2) != to_right
    return jnp.where(swapped, pltpu.roll(chunk, MIRROR_TILE, 1), chunk)


def gather_kernel(band_ref, block_ref, data_ref, out_ref):
    pairs_each = out_ref.shape[2] // 128
    pairs = out_ref.shape[0] * pairs_each
    rows = out_ref.shape[1]
    left_lanes = lax.broadcasted_iota(jnp.int32, (rows, 128), 1) < MIRROR_TILE

    def one_pair(pair, carry):
        left = half_chunk(data_ref, band_ref[2 * pair], block_ref[2 * pair], 0)
        right = half_chunk(data_ref, band_ref[2 * pair + 1], block_ref[2 * pair + 1], 1)
        start = pl.multiple_of((pair % pairs_each) * 128, 128)
        out_ref[pair // pairs_each, :, pl.ds(start, 128)] = jnp.where(
            left_lanes, left, right
        ).astype(out_ref.dtype)
        return carry

    lax.fori_loop(0, pairs, one_pair, 0, unroll=8)


def gather_tiles(bands, blocks, data, out_shape):
    smem = pl.BlockSpec(memory_space=pltpu.SMEM)
    vmem = pl.BlockSpec(memory_space=pltpu.VMEM)
    return pl.pallas_call(
        gather_kernel,
        out_shape=jax.ShapeDtypeStruct(out_shape, data.dtype),
        in_specs=[smem, smem, vmem],
        out_specs=vmem,
        compiler_params=pltpu.CompilerParams(vmem_limit_bytes=VMEM_GRANT),
        cost_estimate=pl.CostEstimate(flops=0, bytes_accessed=6 << 20, transcendentals=0),
    )(bands, blocks, data)


def collect_kernel(block_ref, valid_ref, data_ref, out_ref, low_ref, *totals):
    bands, rows, length = data_ref.shape
    slots = length // MIRROR_TILE
    lane_half = lax.broadcasted_iota(jnp.int32, (rows, 128), 1) // MIRROR_TILE
    for total in totals:
        total[...] = jnp.zeros_like(total)

    def some_slots(step, carry):
        for turn, total in enumerate(totals):
            slot = step * len(totals) + turn
            block = block_ref[slot]
            side = block % 2
            tile = half_chunk(data_ref, slot // slots, slot % slots, side)
            lanes = lane_half == jnp.where(valid_ref[slot] > 0, side, 2)
            start = pl.multiple_of((block // 2) * 128, 128)
            total[:, pl.ds(start, 128)] += jnp.where(lanes, tile, 0.0)
        return carry

    lax.fori_loop(0, bands * slots // len(totals), some_slots, 0, unroll=2)
    surface = totals[0][...]
    for total in totals[1:]:
        surface = surface + total[...]
    out_ref[...] = surface
    low_ref[...] = surface.astype(low_ref.dtype)


def collect_tiles(blocks, valid, data, length):
    smem = pl.BlockSpec(memory_space=pltpu.SMEM)
    vmem = pl.BlockSpec(memory_space=pltpu.VMEM)
    extent = (data.shape[1], length)
    return pl.pallas_call(
        collect_kernel,
        out_shape=[
            jax.ShapeDtypeStruct(extent, jnp.float32),
            jax.ShapeDtypeStruct(extent, jnp.bfloat16),
        ],
        in_specs=[smem, smem, vmem],
        out_specs=[vmem, vmem],
        scratch_shapes=[pltpu.VMEM(extent, jnp.float32)] * 4,
        compiler_params=pltpu.CompilerParams(vmem_limit_bytes=VMEM_GRANT),
        cost_estimate=pl.CostEstimate(flops=0, bytes_accessed=6 << 20, transcendentals=0),
    )(blocks, valid, data)


def pack_kernel(column_ref, data_ref, *out_refs):
    left_lanes = lax.broadcasted_iota(jnp.int32, (data_ref.shape[1], 128), 1) < MIRROR_TILE
    slots = out_refs[0].shape[1] // MIRROR_TILE
    for turn, out_ref in enumerate(out_refs):
        for slot in range(0, slots, 2):
            at = turn * slots + slot
            left = half_chunk(data_ref, 0, column_ref[at], 0)
            right = half_chunk(data_ref, 0, column_ref[at + 1], 1)
            out_ref[:, pl.ds(slot * MIRROR_TILE, 128)] = jnp.where(
                left_lanes, left, right
            ).astype(out_ref.dtype)


def collect_blocks_kernel(count, block_ref, valid_ref, *refs):
    data_refs, (out_ref, low_ref), totals = refs[:count], refs[count : count + 2], refs[count + 2 :]
    rows, width = data_refs[0].shape
    slots = width // MIRROR_TILE
    lane_half = lax.broadcasted_iota(jnp.int32, (rows, 128), 1) // MIRROR_TILE
    for total in totals:
        total[...] = jnp.zeros_like(total)
    for turn, data_ref in enumerate(data_refs):
        for slot in range(slots):
            total = totals[slot % len(totals)]
            block = block_ref[turn * slots + slot]
            side = block % 2
            chunk = data_ref[:, pl.ds(slot // 2 * 128, 128)].astype(jnp.float32)
            tile = jnp.where(side != slot % 2, pltpu.roll(chunk, MIRROR_TILE, 1), chunk)
            lanes = lane_half == jnp.where(valid_ref[turn * slots + slot] > 0, side, 2)
            start = pl.multiple_of((block // 2) * 128, 128)
            total[:, pl.ds(start, 128)] += jnp.where(lanes, tile, 0.0)
    surface = totals[0][...]
    for total in totals[1:]:
        surface = surface + total[...]
    out_ref[...] = surface
    low_ref[...] = surface.astype(low_ref.dtype)


def return_by_permutes(beam, columns, blocks, valid, length):
    bands, slots = columns.shape
    rows = beam.shape[1]
    me = lax.axis_index("band")
    steps = jnp.arange(bands, dtype=jnp.int32)
    ahead = jnp.take(columns, (me + steps) % bands, axis=0).reshape(-1)
    behind = (me - steps + bands) % bands
    smem = pl.BlockSpec(memory_space=pltpu.SMEM)
    vmem = pl.BlockSpec(memory_space=pltpu.VMEM)
    parts = pl.pallas_call(
        pack_kernel,
        out_shape=[jax.ShapeDtypeStruct((rows, slots * MIRROR_TILE), beam.dtype)] * bands,
        in_specs=[smem, vmem],
        out_specs=[vmem] * bands,
        compiler_params=pltpu.CompilerParams(vmem_limit_bytes=VMEM_GRANT),
        cost_estimate=pl.CostEstimate(flops=0, bytes_accessed=2 << 20, transcendentals=0),
    )(ahead, beam)
    arrived = [parts[0]]
    for step in range(1, bands):
        ring = [(i, (i + step) % bands) for i in range(bands)]
        arrived.append(lax.ppermute(parts[step], "band", ring))
    extent = (rows, length)
    return pl.pallas_call(
        functools.partial(collect_blocks_kernel, bands),
        out_shape=[
            jax.ShapeDtypeStruct(extent, jnp.float32),
            jax.ShapeDtypeStruct(extent, jnp.bfloat16),
        ],
        in_specs=[smem, smem] + [vmem] * bands,
        out_specs=[vmem, vmem],
        scratch_shapes=[pltpu.VMEM(extent, jnp.float32)] * 4,
        compiler_params=pltpu.CompilerParams(vmem_limit_bytes=VMEM_GRANT),
        cost_estimate=pl.CostEstimate(flops=0, bytes_accessed=2 << 20, transcendentals=0),
    )(
        jnp.take(blocks, behind, axis=0).reshape(-1),
        jnp.take(valid, behind, axis=0).reshape(-1),
        *arrived,
    )


def approach_kernel(real_ref, imag_ref, weight_ref, *out_refs):
    tile = weight_ref.shape[0] // 2
    at = pl.multiple_of(pl.program_id(0) * tile, tile)
    lines = jnp.concatenate(
        [real_ref[:, pl.ds(at, 3 * tile)], imag_ref[:, pl.ds(at, 3 * tile)]], axis=1
    )
    turned = lax.dot_general(
        weight_ref[...], lines, (((1,), (1,)), ((), ())), preferred_element_type=jnp.float32
    ).astype(out_refs[0].dtype)
    for half in range(lines.shape[0] // tile):
        for part in range(2):
            first = part * tile
            for out_ref in out_refs:
                last = first + out_ref.shape[1]
                out_ref[0, :, pl.ds((2 * half + part) * tile, tile)] = turned[
                    first:last, half * tile : (half + 1) * tile
                ]
                first = last


def approach_turned(real_lines, imag_lines, weight, modes, bands, chunks):
    rows = real_lines.shape[0]
    tile = weight.shape[0] // 2
    tiles = modes * bands
    return pl.pallas_call(
        approach_kernel,
        out_shape=[jax.ShapeDtypeStruct((tiles, each, 2 * rows), jnp.bfloat16) for each in chunks],
        grid=(tiles,),
        in_specs=[
            pl.BlockSpec(real_lines.shape, lambda t: (0, 0)),
            pl.BlockSpec(imag_lines.shape, lambda t: (0, 0)),
            pl.BlockSpec(weight.shape, lambda t: (0, 0)),
        ],
        out_specs=[
            pl.BlockSpec(
                (1, each, 2 * rows), lambda t: ((t % modes) * bands + t // modes, 0, 0)
            )
            for each in chunks
        ],
        compiler_params=pltpu.CompilerParams(vmem_limit_bytes=VMEM_GRANT),
        cost_estimate=pl.CostEstimate(
            flops=2 * rows * weight.size * tiles, bytes_accessed=8 << 20, transcendentals=0
        ),
    )(real_lines, imag_lines, weight)


def beam_kernel(
    modes, first, moved_ref, cos_ref, sin_ref, target_ref, approach_ref, focus_ref, adjoint_ref,
    sens_ref, lines, screens, grads, sems,
):
    sources, rows, width = moved_ref.shape
    bands = sources // modes
    tile = focus_ref.shape[1] // 2
    pair = 2 * tile
    tiles = cos_ref.shape[1] // tile

    def fetch(index):
        mode, band = index // bands, index % bands
        return pltpu.make_async_copy(
            moved_ref.at[index],
            lines.at[pl.ds(mode * rows, rows), pl.ds(pair + band * width, width)],
            sems.at[index],
        )

    for index in range(sources):
        fetch(index).start()
    edge = jnp.zeros((lines.shape[0], pair), lines.dtype)
    screens[:, pl.ds(0, pair)] = edge
    screens[:, pl.ds((tiles + 1) * pair, pair)] = edge
    grads[:, pl.ds(0, pair)] = edge
    grads[:, pl.ds((tiles + 1) * pair, pair)] = edge
    lines[:, pl.ds(0, pair)] = edge
    lines[:, pl.ds((tiles + 1) * pair, pair)] = edge
    for index in range(sources):
        fetch(index).wait()

    def window(ref, at):
        return ref[:, pl.ds(pl.multiple_of(at * pair, pair), 3 * pair)]

    def put(ref, at, value):
        ref[:, pl.ds(pl.multiple_of((at + 1) * pair, pair), pair)] = value

    def columns(ref, at):
        return ref[pl.ds(first, rows), pl.ds(pl.multiple_of(at * tile, tile), tile)]

    group = math.gcd(GROUP, tiles)
    stacked = modes * rows

    def products(ref, first_at, weight_ref):
        windows = jnp.concatenate([window(ref, first_at + turn) for turn in range(group)], axis=0)
        out = jnp.dot(windows, weight_ref[...], preferred_element_type=jnp.float32)
        return [
            (first_at + turn, out[turn * stacked : (turn + 1) * stacked]) for turn in range(group)
        ]

    def mode_sum(value):
        total = value[:rows]
        for mode in range(1, modes):
            total = total + value[mode * rows : (mode + 1) * rows]
        return total

    def screen_step(step, carry):
        for at, advanced in products(lines, step * group, approach_ref):
            advanced = advanced.astype(jnp.bfloat16).astype(jnp.float32)
            cosine = jnp.concatenate([columns(cos_ref, at)] * modes, axis=0)
            sine = jnp.concatenate([columns(sin_ref, at)] * modes, axis=0)
            real, imag = advanced[:, :tile], advanced[:, tile:]
            screened = jnp.concatenate(
                [real * cosine - imag * sine, real * sine + imag * cosine], axis=1
            )
            put(screens, at, screened.astype(jnp.bfloat16))
        return carry

    def detect_step(step, carry):
        for at, detected in products(screens, step * group, focus_ref):
            power = detected * detected
            intensity = mode_sum(power[:, :tile] + power[:, tile:])
            residual = intensity - columns(target_ref, at).astype(jnp.float32)
            residual = jnp.concatenate([residual] * modes, axis=0)
            residual = jnp.concatenate([residual] * 2, axis=1)
            put(grads, at, (detected * residual).astype(jnp.bfloat16))
        return carry

    def sens_step(step, carry):
        for at, grad in products(grads, step * group, adjoint_ref):
            screened = screens[:, pl.ds(pl.multiple_of((at + 1) * pair, pair), pair)]
            screened = screened.astype(jnp.float32)
            terms = grad[:, tile:] * screened[:, :tile] - grad[:, :tile] * screened[:, tile:]
            sens_ref[:, pl.ds(pl.multiple_of(at * tile, tile), tile)] = (
                2.0 * PHASE_FACTOR * mode_sum(terms)
            ).astype(sens_ref.dtype)
        return carry

    lax.fori_loop(0, tiles // group, screen_step, 0)
    lax.fori_loop(0, tiles // group, detect_step, 0)
    lax.fori_loop(0, tiles // group, sens_step, 0)


def beam_sensitivity(first, moved, cosine, sine, target, approach, focus, adjoint, modes):
    rows, length = moved.shape[1], cosine.shape[1]
    vmem = pl.BlockSpec(memory_space=pltpu.VMEM)
    held = pltpu.VMEM((modes * rows, 2 * length + 2 * focus.shape[1]), jnp.bfloat16)
    return pl.pallas_call(
        functools.partial(beam_kernel, modes, first),
        out_shape=jax.ShapeDtypeStruct((rows, length), jnp.bfloat16),
        in_specs=[pl.BlockSpec(memory_space=pl.ANY)] + [vmem] * 6,
        out_specs=vmem,
        scratch_shapes=[held, held, held, pltpu.SemaphoreType.DMA((moved.shape[0],))],
        compiler_params=pltpu.CompilerParams(vmem_limit_bytes=VMEM_GRANT),
        cost_estimate=pl.CostEstimate(
            flops=2 * modes * rows * focus.size * (length // (focus.shape[1] // 2)) * 3,
            bytes_accessed=12 << 20,
            transcendentals=0,
        ),
    )(moved, cosine, sine, target, approach, focus, adjoint)


def join_kernel(counts, owner_ref, *refs):
    out_ref = refs[-1]
    steps = owner_ref.shape[0]
    share = out_ref.shape[0] // steps
    unit = math.gcd(*[ref.shape[0] for ref in refs])
    position = 0
    for step in range(steps):
        first = owner_ref[step] * share
        for ref in refs[position : position + counts[step]]:
            lines = ref.shape[0]
            at = pl.multiple_of(first, unit)
            out_ref[pl.ds(at, lines), :] = ref[...].astype(out_ref.dtype)
            first = first + lines
        position += counts[step]


def join_shares(owners, pieces, rows, length):
    early = [pieces[0]] + [others[:-1] for others in pieces[1:]]
    flat = [piece for step in early for piece in step]
    vmem = pl.BlockSpec(memory_space=pltpu.VMEM)
    joined = pl.pallas_call(
        functools.partial(join_kernel, [len(step) for step in early]),
        out_shape=jax.ShapeDtypeStruct((rows, length), jnp.float32),
        in_specs=[pl.BlockSpec(memory_space=pltpu.SMEM)] + [vmem] * len(flat),
        out_specs=vmem,
        compiler_params=pltpu.CompilerParams(vmem_limit_bytes=VMEM_GRANT),
        cost_estimate=pl.CostEstimate(flops=0, bytes_accessed=8 << 20, transcendentals=0),
    )(owners, *flat)
    share = rows // len(pieces)
    for step in range(1, len(pieces)):
        last = pieces[step][-1].astype(jnp.float32)
        first = (owners[step] + 1) * share - last.shape[0]
        joined = lax.dynamic_update_slice_in_dim(joined, last, first, 0)
    return joined


def fast_shards(mode_field, figure, target, footprint, approach_tiles, focus_tiles):
    modes = lax.axis_size("mode")
    bands = lax.axis_size("band")
    mode_index = lax.axis_index("mode")
    band_index = lax.axis_index("band")
    rows, length = figure.shape
    share = rows // modes
    blocks = length // MIRROR_TILE
    slots = max(2, 2 * blocks // bands)
    chunks = [share * eighths // sum(EIGHTHS) for eighths in EIGHTHS]
    tile = approach_tiles.shape[-1]

    source_band = footprint // blocks
    source_block = footprint % blocks
    column = jnp.arange(blocks, dtype=jnp.int32)
    same = source_band[:, :, None] == source_band[:, None, :]
    rank = jnp.sum((same & (column[None, :] < column[:, None])[None]).astype(jnp.int32), axis=2)
    slot_ids = jnp.arange(slots, dtype=jnp.int32)
    from_here = (source_band == band_index)[:, None, :] & (
        rank[:, None, :] == slot_ids[None, :, None]
    )
    asked_block = jnp.sum(jnp.where(from_here, source_block[:, None, :], 0), axis=2).reshape(-1)
    asked = jnp.sum(from_here.astype(jnp.int32), axis=2).reshape(-1)
    my_band = lax.dynamic_index_in_dim(source_band, band_index, 0, keepdims=False)
    my_rank = lax.dynamic_index_in_dim(rank, band_index, 0, keepdims=False)
    band_ids = jnp.arange(bands, dtype=jnp.int32)
    mine = (my_band[None, None, :] == band_ids[:, None, None]) & (
        my_rank[None, None, :] == slot_ids[None, :, None]
    )
    back_column = jnp.sum(jnp.where(mine, column[None, None, :], 0), axis=2).reshape(-1)
    no_band = jnp.zeros_like(asked_block)

    packed = (bands, share, slots * MIRROR_TILE)
    heights = lax.dynamic_slice_in_dim(figure, mode_index * share, share, 0)[None]
    outbound = gather_tiles(no_band, asked_block, heights, packed)
    inbound = lax.all_to_all(outbound, "band", split_axis=0, concat_axis=0, tiled=True)

    approach = real_kernels(approach_tiles)
    focus = real_kernels(focus_tiles)
    adjoint = jnp.transpose(focus, (0, 3, 4, 1, 2))[::-1]
    flat = (3 * 2 * tile, 2 * tile)
    turned_weight = jnp.transpose(approach, (3, 4, 1, 0, 2)).reshape(2 * tile, 3 * 2 * tile)
    edges = ((0, 0), (tile, tile))
    real_lines = jnp.pad(mode_field[0, :, 0], edges)
    imag_lines = jnp.pad(mode_field[0, :, 1], edges)
    turned = approach_turned(real_lines, imag_lines, turned_weight, modes, bands, chunks)
    def to_all(part):
        return lax.all_to_all(part, ("mode", "band"), split_axis=0, concat_axis=0, tiled=True)

    moved = [to_all(turned[0])]

    heights_here = gather_tiles(my_band, my_rank, inbound, (1, share, length))[0]
    phase_delay = PHASE_FACTOR * heights_here.astype(jnp.float32)
    beside = (
        jnp.cos(phase_delay),
        jnp.sin(phase_delay),
        lax.dynamic_slice_in_dim(target, mode_index * share, share, 0),
        approach.reshape(flat),
        focus.reshape(flat),
        adjoint.reshape(flat),
    )
    later, beside = lax.optimization_barrier((turned[1:], beside))
    moved += [to_all(part) for part in later]

    pieces = [[] for step in range(modes)]
    first = 0
    for each, lines in zip(chunks, moved):
        beam = beam_sensitivity(first, lines, *beside, modes)
        first += each
        packed_part = (bands, each, slots * MIRROR_TILE)
        if first < share:
            back = gather_tiles(no_band, back_column, beam[None], packed_part)
            returned = lax.all_to_all(back, "band", split_axis=0, concat_axis=0, tiled=True)
            surface, low = collect_tiles(asked_block, asked, returned, length)
        else:
            tables = [t.reshape(bands, slots) for t in (back_column, asked_block, asked)]
            surface, low = return_by_permutes(beam[None], *tables, length)
        pieces[0].append(surface)
        for step in range(1, modes):
            ring = [(i, (i + step) % modes) for i in range(modes)]
            pieces[step].append(lax.ppermute(low, "mode", ring))
    owners = jnp.remainder(mode_index - jnp.arange(modes, dtype=jnp.int32), modes)
    return join_shares(owners.astype(jnp.int32), pieces, rows, length)


def solution(mesh):
    modes, bands = mesh.shape["mode"], mesh.shape["band"]

    def shards(mode_field, figure, target, footprint, approach_tiles, focus_tiles):
        tile = approach_tiles.shape[-1]
        share = figure.shape[0] // modes
        fits = mode_field.shape[0] == 1 and share == tile and figure.shape[0] % tile == 0
        fits = fits and tile == 2 * MIRROR_TILE and figure.shape[1] == modes * bands * tile
        chosen = fast_shards if fits else general_shards
        return chosen(mode_field, figure, target, footprint, approach_tiles, focus_tiles)

    in_specs = (P("mode", "band", None, None), P("band", None), P("band", None), P(), P(), P())
    out_specs = P("band", None)
    return jax.shard_map(shards, mesh=mesh, in_specs=in_specs, out_specs=out_specs, check_vma=False)
```
